512 devices in a mesh: lat: 32 (over x, y), chan: 16 (over z, core).
Axes of the slice: x: 4, y: 8, z: 8, core: 2. Of those that a mesh axis runs over, the one named last changes fastest.
Arguments:
- grid_field: bfloat16 [512, 128, 1440], P('lat', 'chan'), may hold values from -6 to 6
- legendre: bfloat16 [512, 192, 385], P(None, 'lat'), may hold values from -0.25 to 0.25
- mix_weight: bfloat16 [2, 128, 128], P(None, 'chan'), may hold values from -0.375 to 0.375
- pair_order: int32 [192], replicated, may hold values from 0 to 191, each once
Outputs:
- mixed_coeffs: bfloat16 [192, 2, 128, 385], P('lat', None, 'chan')
The draws below stay inside these ranges and needn't reach their ends.
Inputs may be any that keep to these rules, and one draw needn't show every extreme that they name: `pair_order`: each pair 0 to 191 stands at exactly one position.
All inputs are finite; a program needn't handle non-finite values.
Results may differ from the reference program's by a relative error of at most 0.025.
Values may be sent and summed in bfloat16 or wider, within the bound.
A program may use at most 64 MiB of HBM per device.

```python
import math
import jax
import jax.numpy as jnp
from jax import lax

NLON = 1440
LMAX = 384
CHANNELS = 128
LAT_DEV = 16
PAIRS = 192
NLAT = 512
N_LAT = 32


def shard_levels(key, extent, pieces, low, largest):
    def one(position, parts):
        draws = jax.random.uniform(jax.random.fold_in(jax.random.fold_in(key, 6), position), (parts,), jnp.float32, low / len(pieces), largest / len(pieces))
        return jnp.repeat(jnp.exp(draws), extent[position] // parts).reshape((-1,) + (1,) * (len(extent) - position - 1))

    gain = one(*pieces[0])
    for cut in pieces[1:]:
        gain = gain * one(*cut)
    return gain


def noise(stream_key, dims, deviation, reach, split=(), kind=jnp.bfloat16):
    entries = jax.random.normal(stream_key, dims, jnp.float32) * deviation
    if len(split) > 0:
        entries = shard_levels(stream_key, dims, split, -0.22, 0.18) * entries
    return jnp.clip(entries, min=-reach, max=reach).astype(kind)


def setup_inputs(seed: int = 0) -> dict:
    arg_keys = jax.random.split(jax.random.key(seed), 5)
    grid_field = noise(arg_keys[0], (NLAT, CHANNELS, NLON), 1.0, 6.0, ((0, 32), (1, 16)))
    legendre = noise(arg_keys[1], (NLAT, PAIRS, LMAX + 1), NLAT ** -0.5, 0.25, ((1, 32),))
    mix_weight = noise(arg_keys[2], (2, CHANNELS, CHANNELS), (2 * CHANNELS) ** -0.5, 0.375, ((1, 16),))
    pair_order = jax.random.permutation(arg_keys[3], PAIRS).astype(jnp.int32)
    return {"grid_field": grid_field, "legendre": legendre, "mix_weight": mix_weight, "pair_order": pair_order}


def fourier_tables(lon_count, order_count):
    orders = lax.broadcasted_iota(jnp.int32, (lon_count, order_count), 1)
    columns = lax.broadcasted_iota(jnp.int32, (lon_count, order_count), 0)
    phases = 2.0 * math.pi / lon_count * (orders * columns % lon_count).astype(jnp.float32)
    return (jnp.cos(phases).astype(jnp.bfloat16), jnp.sin(phases).astype(jnp.bfloat16))

def reference(grid_field, legendre, mix_weight, pair_order):
    cosine, sine_table = fourier_tables(NLON, LMAX)
    flat_field = grid_field.reshape(NLAT * CHANNELS, NLON)
    real_part = jnp.dot(flat_field, cosine, preferred_element_type=jnp.float32) / math.sqrt(NLON)
    imag_part = -jnp.dot(flat_field, sine_table, preferred_element_type=jnp.float32) / math.sqrt(NLON)
    spectrum = jnp.stack([real_part.reshape(NLAT, CHANNELS, LMAX), imag_part.reshape(NLAT, CHANNELS, LMAX)], axis=1).astype(jnp.bfloat16)
    first_order = jnp.take(spectrum, pair_order, axis=3)
    second_order = jnp.take(spectrum, LMAX - 1 - pair_order, axis=3)
    slot_ids = jnp.arange(LMAX + 1, dtype=jnp.int32)
    slot_mask = slot_ids[None, :] < (LMAX - pair_order)[:, None]

    def add_band(running, band_index):
        start_row = band_index * LAT_DEV
        table_band = lax.dynamic_slice_in_dim(legendre, start_row, LAT_DEV, 0).astype(jnp.float32)
        first_band = lax.dynamic_slice_in_dim(first_order, start_row, LAT_DEV, 0).astype(jnp.float32)
        second_band = lax.dynamic_slice_in_dim(second_order, start_row, LAT_DEV, 0).astype(jnp.float32)
        with_first = jnp.einsum('lkn,lrck->krcn', table_band, first_band)
        with_second = jnp.einsum('lkn,lrck->krcn', table_band, second_band)
        chosen = jnp.where(slot_mask[:, None, None, :], with_first, with_second)
        rounded = lax.optimization_barrier(chosen.astype(jnp.bfloat16))
        return (running + rounded.astype(running.dtype), band_index)
    initial = jnp.zeros((PAIRS, 2, CHANNELS, LMAX + 1), jnp.float32)
    summed, ignored = lax.scan(add_band, initial, jnp.arange(N_LAT, dtype=jnp.int32))
    coeffs = summed.astype(jnp.bfloat16).astype(jnp.float32)
    weights = mix_weight.astype(jnp.float32)
    real_in = coeffs[:, 0]
    imag_in = coeffs[:, 1]
    real_out = jnp.einsum('oc,kcn->kon', weights[0], real_in) - jnp.einsum('oc,kcn->kon', weights[1], imag_in)
    imag_out = jnp.einsum('oc,kcn->kon', weights[0], imag_in) + jnp.einsum('oc,kcn->kon', weights[1], real_in)
    return jnp.stack([real_out, imag_out], axis=1).astype(jnp.bfloat16)
```

```python
import math

import jax
import jax.numpy as jnp
import ml_dtypes
import numpy as np
from jax import lax
from jax.sharding import PartitionSpec as P


def fourier_table(lon_count, order_count):
    orders = np.arange(order_count, dtype=np.int32)[None, :]
    columns = np.arange(lon_count, dtype=np.int32)[:, None]
    phases = np.float32(2.0 * math.pi / lon_count) * ((orders * columns) % lon_count).astype(np.float32)
    table = np.concatenate([np.cos(phases), -np.sin(phases)], axis=1)
    return table.astype(ml_dtypes.bfloat16)


def body(grid_field, legendre, mix_weight, pair_order):
    lat_rows, chan_cols, lon_count = grid_field.shape
    pair_rows, slot_count = legendre.shape[1:]
    order_count = slot_count - 1
    table = jnp.asarray(fourier_table(lon_count, order_count))
    flat_field = grid_field.reshape(lat_rows * chan_cols, lon_count)
    spectrum = (
        jnp.dot(flat_field, table, preferred_element_type=jnp.float32) / math.sqrt(lon_count)
    ).astype(jnp.bfloat16)
    spectrum = spectrum.reshape(lat_rows, chan_cols, 2, order_count)
    both = jnp.stack([pair_order, order_count - 1 - pair_order], axis=1).reshape(-1)
    picked = jnp.take(spectrum, both, axis=3)
    moved = lax.all_to_all(picked, "lat", split_axis=3, concat_axis=0, tiled=True)
    lat_count = moved.shape[0]
    moved = moved.reshape(lat_count, chan_cols, 2, pair_rows, 2)
    mine = lax.dynamic_slice_in_dim(pair_order, lax.axis_index("lat") * pair_rows, pair_rows)
    slot_ids = lax.broadcasted_iota(jnp.int32, (pair_rows, slot_count), 1)
    slot_mask = slot_ids < (order_count - mine)[:, None]
    sums = jnp.einsum("tkn,tcrkh->khrcn", legendre, moved, preferred_element_type=jnp.float32)
    summed = jnp.where(slot_mask[:, None, None, :], sums[:, 0], sums[:, 1]).astype(jnp.bfloat16)
    pieces = lax.all_gather(summed, "chan", axis=2, tiled=True)
    channels = pieces.shape[2]
    w_real, w_imag = mix_weight[0], mix_weight[1]
    weights = jnp.stack(
        [jnp.stack([w_real, -w_imag], axis=1), jnp.stack([w_imag, w_real], axis=1)], axis=0
    ).reshape(2 * chan_cols, 2 * channels)
    mixed = jnp.einsum(
        "oc,kcn->kon",
        weights,
        pieces.reshape(pair_rows, 2 * channels, slot_count),
        preferred_element_type=jnp.float32,
    )
    return mixed.reshape(pair_rows, 2, chan_cols, slot_count).astype(jnp.bfloat16)


def solution(mesh):
    return jax.shard_map(
        body,
        mesh=mesh,
        in_specs=(P("lat", "chan", None), P(None, "lat", None), P(None, "chan", None), P()),
        out_specs=P("lat", None, "chan", None),
        check_vma=False,
    )
```

```python
import functools
import math

import jax
import jax.numpy as jnp
import ml_dtypes
import numpy as np
from jax import lax
from jax.experimental import pallas as pl
from jax.experimental.pallas import tpu as pltpu
from jax.sharding import PartitionSpec as P

BF16 = jnp.bfloat16
F32 = jnp.float32
NX, NY, NZ = 4, 8, 8
N_LAT, N_CHAN = NX * NY, 2 * NZ
LAT, CH, NLON = 16, 8, 1440
ORDERS, SLOTS, PAIRS, MINE = 384, 385, 192, 6
ROWS = 4 * MINE
UNITS = 19
EXTRA = (0, 6, 10)
MESH = pl.DeviceIdType.MESH
NT = (((1,), (1,)), ((), ()))


def fourier_table():
    orders = np.arange(ORDERS, dtype=np.int32)[:, None]
    columns = np.arange(NLON, dtype=np.int32)[None, :]
    phases = np.float32(2.0 * math.pi / NLON) * ((orders * columns) % NLON).astype(np.float32)
    return np.concatenate([np.cos(phases), -np.sin(phases)], axis=0).astype(ml_dtypes.bfloat16)


def constants():
    row = np.arange(N_LAT * ROWS)
    part, half, pair = (row // 12) % 2, (row // 6) % 2, (row // ROWS) * MINE + row % MINE
    pick = np.zeros((row.size, PAIRS), np.float32)
    pick[row, pair] = 1 - 2 * half
    base = np.broadcast_to((part * ORDERS + half * (ORDERS - 1))[:, None], (row.size, 128))
    s, t, c = np.meshgrid(np.arange(8), np.arange(LAT), np.arange(CH), indexing="ij")
    regroup = np.zeros((1024, 1024), np.float32)
    regroup[(s * 128 + t * CH + c).ravel(), (c * 128 + s * LAT + t).ravel()] = 1
    lane = np.arange(CH * ROWS)
    pair_lane = np.broadcast_to((lane % MINE)[None, :], (8, lane.size)).astype(np.int32)
    k, r, c = np.meshgrid(np.arange(MINE), np.arange(2), np.arange(CH), indexing="ij")
    fold = np.zeros((2, MINE * 16, CH * ROWS), np.float32)
    for half in range(2):
        fold[half, (k * 16 + r * 8 + c).ravel(), (c * ROWS + r * 12 + half * MINE + k).ravel()] = 1
    out_row = np.arange(MINE * 16)
    offset = (np.arange(PAIRS)[None, :] - (out_row // 16)[:, None]).astype(np.int32)
    bf = ml_dtypes.bfloat16
    return (
        fourier_table(),
        pick.astype(bf),
        base.astype(np.float32),
        regroup.astype(bf),
        pair_lane,
        fold.astype(bf),
        offset,
    )


def kernel(
    x_hbm, leg_hbm, mix_hbm, order_hbm, table_hbm, pick_hbm, base_hbm, regroup_hbm, lane_hbm, fold_hbm,
    offset_hbm, out_ref,
    x, leg, order, table, pick, base, regroup, lane, fold, offset,
    send, recv, weights, units, gathered, mixed, back,
    local_sem, lat_send, lat_recv, w_send, w_recv, c_send, c_recv, m_send, m_recv,
):
    li, ci = lax.axis_index("lat"), lax.axis_index("chan")
    lx, ly = li // NY, li % NY
    cz, cc = ci // 2, ci % 2

    def lat_peer(step):
        return lax.rem(lx + step // NY, NX) * NY + lax.rem(ly + step % NY, NY)

    def chan_peer(step):
        return lax.rem(cz + step // 2, NZ) * 2 + lax.rem(cc + step % 2, 2)

    barrier = pltpu.get_barrier_semaphore()

    @pl.loop(1, N_LAT)
    def _(step):
        pl.semaphore_signal(barrier, inc=1, device_id=(lat_peer(step), ci), device_id_type=MESH)

    @pl.loop(1, N_CHAN)
    def _(step):
        pl.semaphore_signal(barrier, inc=1, device_id=(li, chan_peer(step)), device_id_type=MESH)

    loads = [
        pltpu.make_async_copy(src, dst, local_sem.at[i])
        for i, (src, dst) in enumerate(
            [
                (order_hbm, order), (pick_hbm, pick), (base_hbm, base), (x_hbm, x), (table_hbm, table),
                (mix_hbm, weights.at[ci]), (regroup_hbm, regroup), (leg_hbm, leg), (lane_hbm, lane),
                (fold_hbm, fold), (offset_hbm, offset),
            ]
        )
    ]
    for load in loads:
        load.start()
    for load in loads[:3]:
        load.wait()
    order_rows = jnp.broadcast_to(order[...], (128, PAIRS)).astype(F32).astype(BF16)
    key = base[...] + lax.dot_general(pick[...], order_rows, NT, preferred_element_type=F32)
    column = lax.broadcasted_iota(jnp.int32, key.shape, 1).astype(F32)
    place = jnp.concatenate(
        [jnp.where(key == column + 128.0 * b, 1.0, 0.0).astype(BF16) for b in range(2 * ORDERS // 128)],
        axis=1,
    )
    for load in loads[3:5]:
        load.wait()
    spectrum = lax.dot_general(table[...], x[...], NT, preferred_element_type=F32)
    spectrum = (spectrum * (1.0 / math.sqrt(NLON))).astype(BF16)
    placed = jnp.dot(place, spectrum, preferred_element_type=F32)
    send[...] = placed.reshape(N_LAT, ROWS, 128).astype(BF16)

    pl.semaphore_wait(barrier, N_LAT + N_CHAN - 2)

    def lat_copy(dest):
        return pltpu.make_async_remote_copy(
            src_ref=send.at[dest], dst_ref=recv.at[li], send_sem=lat_send.at[dest],
            recv_sem=lat_recv.at[li], device_id=(dest, ci), device_id_type=MESH,
        )

    def lat_arrival(src):
        return pltpu.make_async_remote_copy(
            src_ref=send.at[src], dst_ref=recv.at[src], send_sem=lat_send.at[src],
            recv_sem=lat_recv.at[src], device_id=(src, ci), device_id_type=MESH,
        )

    def w_copy(peer, slot):
        return pltpu.make_async_remote_copy(
            src_ref=weights.at[slot], dst_ref=weights.at[slot], send_sem=w_send.at[peer],
            recv_sem=w_recv.at[slot], device_id=(li, peer), device_id_type=MESH,
        )

    @pl.loop(1, N_LAT)
    def _(step):
        lat_copy(lat_peer(step)).start()

    own = pltpu.make_async_copy(send.at[li], recv.at[li], lat_recv.at[li])
    own.start()
    loads[5].wait()

    @pl.loop(1, N_CHAN)
    def _(step):
        w_copy(chan_peer(step), ci).start()

    for load in loads[6:]:
        load.wait()
    mine = jnp.where(offset[...] == li * MINE, 1.0, 0.0).astype(BF16)
    my_order = lax.dot_general(mine, order_rows, NT, preferred_element_type=F32)
    first = lax.broadcasted_iota(jnp.int32, (MINE * 16, SLOTS), 1).astype(F32) < (
        float(ORDERS) - my_order[:, 0:1]
    )

    own.wait()

    @pl.loop(1, N_LAT)
    def _(step):
        lat_arrival(lat_peer(step)).wait_recv()

    blocks = jnp.concatenate(
        [
            jnp.concatenate([recv[g * 8 + s].astype(F32) for s in range(8)], axis=1)
            for g in range(N_LAT // 8)
        ],
        axis=0,
    ).astype(BF16)
    turned = jnp.dot(blocks, regroup[...], preferred_element_type=F32)
    fields = jnp.concatenate(
        [
            jnp.concatenate(
                [turned[g * ROWS : (g + 1) * ROWS, c * 128 : (c + 1) * 128] for g in range(N_LAT // 8)],
                axis=1,
            )
            for c in range(CH)
        ],
        axis=0,
    ).astype(BF16)
    lanes = jnp.broadcast_to(lane[0:1, :], (SLOTS, CH * ROWS))
    sums = jnp.zeros((SLOTS, CH * ROWS), F32)
    for k in range(MINE):
        one = lax.dot_general(leg[k], fields, NT, preferred_element_type=F32)
        sums = jnp.where(lanes == k, one, sums)
    sums = sums.astype(BF16)
    halves = [lax.dot_general(fold[h], sums, NT, preferred_element_type=F32) for h in range(2)]
    coeffs = jnp.where(first, halves[0], halves[1])
    ends = jnp.zeros((16, 128), F32)
    end_lane = lax.broadcasted_iota(jnp.int32, (16, 128), 1)
    for k in range(MINE):
        piece = coeffs[k * 16 : (k + 1) * 16]
        for b in range(3):
            units[k * 3 + b] = piece[:, b * 128 : (b + 1) * 128].astype(BF16)
        ends = jnp.where(end_lane == k, jnp.broadcast_to(piece[:, ORDERS:], (16, 128)), ends)
    units[UNITS - 1] = ends.astype(BF16)

    def unit_copy(unit, slot, peer, src):
        return pltpu.make_async_remote_copy(
            src_ref=units.at[unit], dst_ref=gathered.at[slot, src], send_sem=c_send.at[unit],
            recv_sem=c_recv.at[slot, src], device_id=(li, peer), device_id_type=MESH,
        )

    def back_copy(unit, slot, peer):
        return pltpu.make_async_remote_copy(
            src_ref=mixed.at[slot, peer], dst_ref=back.at[unit], send_sem=m_send.at[slot, peer],
            recv_sem=m_recv.at[unit], device_id=(li, peer), device_id_type=MESH,
        )

    def keep_unit(unit, slot):
        return pltpu.make_async_copy(units.at[unit], gathered.at[slot, ci], c_recv.at[slot, ci])

    def keep_back(unit, slot):
        return pltpu.make_async_copy(mixed.at[slot, ci], back.at[unit], m_recv.at[unit])

    for e, owner in enumerate(EXTRA):

        @pl.when(ci != owner)
        def _():
            unit_copy(16 + e, 1, owner, ci).start()

        @pl.when(ci == owner)
        def _():
            keep_unit(16 + e, 1).start()

    @pl.loop(1, N_CHAN)
    def _(step):
        peer = chan_peer(step)
        unit_copy(peer, 0, peer, ci).start()

    keep_unit(ci, 0).start()

    @pl.loop(1, N_CHAN)
    def _(step):
        peer = chan_peer(step)
        w_copy(peer, peer).wait_recv()

    every = weights[...].astype(F32).reshape(N_CHAN, 2, CH, 128)
    w_real = every[:, 0].reshape(128, 128)
    w_imag = every[:, 1].reshape(128, 128)
    to_real = jnp.concatenate([w_real, -w_imag], axis=1).astype(BF16)
    to_imag = jnp.concatenate([w_imag, w_real], axis=1).astype(BF16)

    def mix(slot, unit):
        keep_unit(unit, slot).wait()

        @pl.loop(1, N_CHAN)
        def _(step):
            peer = chan_peer(step)
            unit_copy(unit, slot, peer, peer).wait_recv()

        both = gathered[slot].astype(F32).reshape(N_CHAN, 2, CH, 128)
        both = jnp.concatenate(
            [both[:, 0].reshape(128, 128), both[:, 1].reshape(128, 128)], axis=0
        ).astype(BF16)
        real = jnp.dot(to_real, both, preferred_element_type=F32).reshape(N_CHAN, CH, 128)
        imag = jnp.dot(to_imag, both, preferred_element_type=F32).reshape(N_CHAN, CH, 128)
        mixed[slot] = jnp.concatenate([real, imag], axis=1).astype(BF16)

        @pl.loop(1, N_CHAN)
        def _(step):
            back_copy(unit, slot, chan_peer(step)).start()

        keep_back(unit, slot).start()

    for e, owner in enumerate(EXTRA):

        @pl.when(ci == owner)
        def _():
            mix(1, 16 + e)

    mix(0, ci)

    @pl.loop(1, N_CHAN)
    def _(step):
        peer = chan_peer(step)
        back_copy(peer, 0, peer).wait_recv()

    keep_back(ci, 0).wait()
    for e, owner in enumerate(EXTRA):

        @pl.when(ci != owner)
        def _():
            back_copy(16 + e, 1, owner).wait_recv()

        @pl.when(ci == owner)
        def _():
            keep_back(16 + e, 1).wait()

    last = back[UNITS - 1].astype(F32)
    for k in range(MINE):
        out_ref[k] = jnp.concatenate(
            [back[k * 3 + b].astype(F32) for b in range(3)] + [last[:, k : k + 1]], axis=1
        ).astype(BF16)

    @pl.loop(1, N_LAT)
    def _(step):
        lat_copy(lat_peer(step)).wait_send()

    @pl.loop(1, N_CHAN)
    def _(step):
        peer = chan_peer(step)
        w_copy(peer, ci).wait_send()
        unit_copy(peer, 0, peer, ci).wait_send()
        back_copy(ci, 0, peer).wait_send()

    for e, owner in enumerate(EXTRA):

        @pl.when(ci != owner)
        def _():
            unit_copy(16 + e, 1, owner, ci).wait_send()

        @pl.when(ci == owner)
        def _():
            @pl.loop(1, N_CHAN)
            def _(step):
                back_copy(16 + e, 1, chan_peer(step)).wait_send()


def body(grid_field, legendre, mix_weight, pair_order):
    any_spec = pl.BlockSpec(memory_space=pl.ANY)
    dma = pltpu.SemaphoreType.DMA
    fixed = [jnp.asarray(c) for c in constants()]
    out = pl.pallas_call(
        kernel,
        out_shape=jax.ShapeDtypeStruct((MINE, 16, SLOTS), BF16),
        in_specs=[any_spec] * 11,
        out_specs=pl.BlockSpec(memory_space=pltpu.VMEM),
        scratch_shapes=[
            pltpu.VMEM((LAT * CH, NLON), BF16),
            pltpu.VMEM((MINE, SLOTS, N_LAT * LAT), BF16),
            pltpu.VMEM((1, PAIRS), jnp.int32),
            pltpu.VMEM((2 * ORDERS, NLON), BF16),
            pltpu.VMEM((N_LAT * ROWS, PAIRS), BF16),
            pltpu.VMEM((N_LAT * ROWS, 128), F32),
            pltpu.VMEM((1024, 1024), BF16),
            pltpu.VMEM((8, CH * ROWS), jnp.int32),
            pltpu.VMEM((2, MINE * 16, CH * ROWS), BF16),
            pltpu.VMEM((MINE * 16, PAIRS), jnp.int32),
            pltpu.VMEM((N_LAT, ROWS, 128), BF16),
            pltpu.VMEM((N_LAT, ROWS, 128), BF16),
            pltpu.VMEM((N_CHAN, 16, 128), BF16),
            pltpu.VMEM((UNITS, 16, 128), BF16),
            pltpu.VMEM((2, N_CHAN, 16, 128), BF16),
            pltpu.VMEM((2, N_CHAN, 16, 128), BF16),
            pltpu.VMEM((UNITS, 16, 128), BF16),
            dma((11,)),
            dma((N_LAT,)),
            dma((N_LAT,)),
            dma((N_CHAN,)),
            dma((N_CHAN,)),
            dma((UNITS,)),
            dma((2, N_CHAN)),
            dma((2, N_CHAN)),
            dma((UNITS,)),
        ],
        compiler_params=pltpu.CompilerParams(
            collective_id=0, has_side_effects=True, vmem_limit_bytes=48 * 1024 * 1024
        ),
    )(
        grid_field.reshape(LAT * CH, NLON),
        jnp.transpose(legendre, (1, 2, 0)),
        mix_weight.reshape(16, 128),
        pair_order.reshape(1, PAIRS),
        *fixed,
    )
    return out.reshape(MINE, 2, CH, SLOTS)


def solution(mesh):
    return jax.shard_map(
        body,
        mesh=mesh,
        in_specs=(P("lat", "chan", None), P(None, "lat", None), P(None, "chan", None), P()),
        out_specs=P("lat", None, "chan", None),
        check_vma=False,
    )
```

```python
import math

import jax
import jax.numpy as jnp
import ml_dtypes
import numpy as np
from jax import lax
from jax.experimental import pallas as pl
from jax.experimental.pallas import tpu as pltpu
from jax.sharding import PartitionSpec as P

BF16 = jnp.bfloat16
F32 = jnp.float32
NX, NY, NZ = 4, 8, 8
N_LAT, N_CHAN = NX * NY, 2 * NZ
LAT, CH, NLON = 16, 8, 1440
ORDERS, SLOTS, PAIRS, MINE = 384, 385, 192, 6
ROWS = 4 * MINE
UNITS = 19
EXTRA = (0, 6, 10)
MESH = pl.DeviceIdType.MESH
NT = (((1,), (1,)), ((), ()))


def fourier_table():
    orders = np.arange(ORDERS, dtype=np.int32)[:, None]
    columns = np.arange(NLON, dtype=np.int32)[None, :]
    phases = np.float32(2.0 * math.pi / NLON) * ((orders * columns) % NLON).astype(np.float32)
    return np.concatenate([np.cos(phases), -np.sin(phases)], axis=0).astype(ml_dtypes.bfloat16)


def constants():
    row = np.arange(N_LAT * ROWS)
    part, half, pair = (row // 12) % 2, (row // 6) % 2, (row // ROWS) * MINE + row % MINE
    pick = np.zeros((row.size, PAIRS), np.float32)
    pick[row, pair] = 1 - 2 * half
    base = np.broadcast_to((part * ORDERS + half * (ORDERS - 1))[:, None], (row.size, 128))
    s, t, c = np.meshgrid(np.arange(8), np.arange(LAT), np.arange(CH), indexing="ij")
    regroup = np.zeros((1024, 1024), np.float32)
    regroup[(s * 128 + t * CH + c).ravel(), (c * 128 + s * LAT + t).ravel()] = 1
    lane = np.arange(CH * ROWS)
    pair_lane = np.broadcast_to((lane % MINE)[None, :], (8, lane.size)).astype(np.int32)
    k, r, c = np.meshgrid(np.arange(MINE), np.arange(2), np.arange(CH), indexing="ij")
    fold = np.zeros((2, MINE * 16, CH * ROWS), np.float32)
    for half in range(2):
        fold[half, (k * 16 + r * 8 + c).ravel(), (c * ROWS + r * 12 + half * MINE + k).ravel()] = 1
    out_row = np.arange(MINE * 16)
    offset = (np.arange(PAIRS)[None, :] - (out_row // 16)[:, None]).astype(np.int32)
    bf = ml_dtypes.bfloat16
    return (
        fourier_table(),
        pick.astype(bf),
        base.astype(np.float32),
        regroup.astype(bf),
        pair_lane,
        fold.astype(bf),
        offset,
    )


def kernel(
    x_hbm, leg_hbm, mix_hbm, order_hbm, table_hbm, pick_hbm, base_hbm, regroup_hbm, lane_hbm, fold_hbm,
    offset_hbm, out_ref,
    x, leg, order, table, pick, base, regroup, lane, fold, offset,
    send, recv, weights, units, gathered, mixed, back,
    local_sem, lat_send, lat_recv, w_send, w_recv, c_send, c_recv, m_send, m_recv,
):
    li, ci = lax.axis_index("lat"), lax.axis_index("chan")
    lx, ly = li // NY, li % NY
    cz, cc = ci // 2, ci % 2

    def away(step, ring):
        return ring // 2 + (1 - 2 * (step % 2)) * ((step + 1) // 2)

    def lat_peer(step):
        dx, dy = away(step % NX, NX), away(step // NX, NY)
        return lax.rem(lx + dx, NX) * NY + lax.rem(ly + dy, NY)

    def chan_peer(step):
        return lax.rem(cz + away(step // 2, NZ), NZ) * 2 + lax.rem(cc + 1 - step % 2, 2)

    loads = [
        pltpu.make_async_copy(src, dst, local_sem.at[i])
        for i, (src, dst) in enumerate(
            [
                (order_hbm, order), (pick_hbm, pick), (base_hbm, base), (x_hbm, x), (table_hbm, table),
                (mix_hbm, weights.at[ci]), (offset_hbm, offset), (lane_hbm, lane), (fold_hbm, fold),
                (regroup_hbm, regroup), (leg_hbm, leg),
            ]
        )
    ]
    for load in loads[:5]:
        load.start()

    barrier = pltpu.get_barrier_semaphore()

    @pl.loop(0, N_LAT - 1)
    def _(step):
        pl.semaphore_signal(barrier, inc=1, device_id=(lat_peer(step), ci), device_id_type=MESH)

    @pl.loop(0, N_CHAN - 1)
    def _(step):
        pl.semaphore_signal(barrier, inc=1, device_id=(li, chan_peer(step)), device_id_type=MESH)

    for load in loads[5:]:
        load.start()
    for load in loads[:3]:
        load.wait()
    order_rows = jnp.broadcast_to(order[...], (128, PAIRS)).astype(F32).astype(BF16)
    key = base[...] + lax.dot_general(pick[...], order_rows, NT, preferred_element_type=F32)
    column = lax.broadcasted_iota(jnp.int32, key.shape, 1).astype(F32)
    place = jnp.concatenate(
        [jnp.where(key == column + 128.0 * b, 1.0, 0.0).astype(BF16) for b in range(2 * ORDERS // 128)],
        axis=1,
    )
    for load in loads[3:5]:
        load.wait()
    spectrum = lax.dot_general(table[...], x[...], NT, preferred_element_type=F32)
    spectrum = (spectrum * (1.0 / math.sqrt(NLON))).astype(BF16)
    placed = jnp.dot(place, spectrum, preferred_element_type=F32)
    send[...] = placed.reshape(N_LAT, ROWS, 128).astype(BF16)

    pl.semaphore_wait(barrier, N_LAT + N_CHAN - 2)

    def lat_copy(dest):
        return pltpu.make_async_remote_copy(
            src_ref=send.at[dest], dst_ref=recv.at[li], send_sem=lat_send.at[dest],
            recv_sem=lat_recv.at[li], device_id=(dest, ci), device_id_type=MESH,
        )

    def lat_arrival(src):
        return pltpu.make_async_remote_copy(
            src_ref=send.at[src], dst_ref=recv.at[src], send_sem=lat_send.at[src],
            recv_sem=lat_recv.at[src], device_id=(src, ci), device_id_type=MESH,
        )

    def w_copy(peer, slot):
        return pltpu.make_async_remote_copy(
            src_ref=weights.at[slot], dst_ref=weights.at[slot], send_sem=w_send.at[peer],
            recv_sem=w_recv.at[slot], device_id=(li, peer), device_id_type=MESH,
        )

    @pl.loop(0, N_LAT - 1)
    def _(step):
        lat_copy(lat_peer(step)).start()

    own = pltpu.make_async_copy(send.at[li], recv.at[li], lat_recv.at[li])
    own.start()
    loads[5].wait()

    @pl.loop(0, N_CHAN - 1)
    def _(step):
        w_copy(chan_peer(step), ci).start()

    for load in loads[6:]:
        load.wait()
    mine = jnp.where(offset[...] == li * MINE, 1.0, 0.0).astype(BF16)
    my_order = lax.dot_general(mine, order_rows, NT, preferred_element_type=F32)
    first = lax.broadcasted_iota(jnp.int32, (MINE * 16, SLOTS), 1).astype(F32) < (
        float(ORDERS) - my_order[:, 0:1]
    )

    own.wait()

    @pl.loop(0, N_LAT - 1)
    def _(step):
        lat_arrival(lat_peer(step)).wait_recv()

    blocks = jnp.concatenate(
        [
            jnp.concatenate([recv[g * 8 + s].astype(F32) for s in range(8)], axis=1)
            for g in range(N_LAT // 8)
        ],
        axis=0,
    ).astype(BF16)
    turned = jnp.dot(blocks, regroup[...], preferred_element_type=F32)
    fields = jnp.concatenate(
        [
            jnp.concatenate(
                [turned[g * ROWS : (g + 1) * ROWS, c * 128 : (c + 1) * 128] for g in range(N_LAT // 8)],
                axis=1,
            )
            for c in range(CH)
        ],
        axis=0,
    ).astype(BF16)
    lanes = jnp.broadcast_to(lane[0:1, :], (SLOTS, CH * ROWS))
    sums = jnp.zeros((SLOTS, CH * ROWS), F32)
    for k in range(MINE):
        one = lax.dot_general(leg[k], fields, NT, preferred_element_type=F32)
        sums = jnp.where(lanes == k, one, sums)
    sums = sums.astype(BF16)
    halves = [lax.dot_general(fold[h], sums, NT, preferred_element_type=F32) for h in range(2)]
    coeffs = jnp.where(first, halves[0], halves[1])
    ends = jnp.zeros((16, 128), F32)
    end_lane = lax.broadcasted_iota(jnp.int32, (16, 128), 1)
    for k in range(MINE):
        piece = coeffs[k * 16 : (k + 1) * 16]
        for b in range(3):
            units[k * 3 + b] = piece[:, b * 128 : (b + 1) * 128].astype(BF16)
        ends = jnp.where(end_lane == k, jnp.broadcast_to(piece[:, ORDERS:], (16, 128)), ends)
    units[UNITS - 1] = ends.astype(BF16)

    def unit_copy(unit, slot, peer, src):
        return pltpu.make_async_remote_copy(
            src_ref=units.at[unit], dst_ref=gathered.at[slot, src], send_sem=c_send.at[unit],
            recv_sem=c_recv.at[slot, src], device_id=(li, peer), device_id_type=MESH,
        )

    def back_copy(unit, slot, peer):
        return pltpu.make_async_remote_copy(
            src_ref=mixed.at[slot, peer], dst_ref=back.at[unit], send_sem=m_send.at[slot, peer],
            recv_sem=m_recv.at[unit], device_id=(li, peer), device_id_type=MESH,
        )

    def keep_unit(unit, slot):
        return pltpu.make_async_copy(units.at[unit], gathered.at[slot, ci], c_recv.at[slot, ci])

    def keep_back(unit, slot):
        return pltpu.make_async_copy(mixed.at[slot, ci], back.at[unit], m_recv.at[unit])

    for e, owner in enumerate(EXTRA):

        @pl.when(ci != owner)
        def _():
            unit_copy(16 + e, 1, owner, ci).start()

        @pl.when(ci == owner)
        def _():
            keep_unit(16 + e, 1).start()

    @pl.loop(0, N_CHAN - 1)
    def _(step):
        peer = chan_peer(step)
        unit_copy(peer, 0, peer, ci).start()

    keep_unit(ci, 0).start()

    @pl.loop(0, N_CHAN - 1)
    def _(step):
        peer = chan_peer(step)
        w_copy(peer, peer).wait_recv()

    @pl.loop(0, N_LAT - 1)
    def _(step):
        lat_copy(lat_peer(step)).wait_send()

    @pl.loop(0, N_CHAN - 1)
    def _(step):
        w_copy(chan_peer(step), ci).wait_send()

    every = weights[...].astype(F32).reshape(N_CHAN, 2, CH, 128)
    w_real = every[:, 0].reshape(128, 128)
    w_imag = every[:, 1].reshape(128, 128)
    to_real = jnp.concatenate([w_real, -w_imag], axis=1).astype(BF16)
    to_imag = jnp.concatenate([w_imag, w_real], axis=1).astype(BF16)

    def mix(slot, unit):
        keep_unit(unit, slot).wait()

        @pl.loop(0, N_CHAN - 1)
        def _(step):
            peer = chan_peer(step)
            unit_copy(unit, slot, peer, peer).wait_recv()

        both = gathered[slot].astype(F32).reshape(N_CHAN, 2, CH, 128)
        both = jnp.concatenate(
            [both[:, 0].reshape(128, 128), both[:, 1].reshape(128, 128)], axis=0
        ).astype(BF16)
        real = jnp.dot(to_real, both, preferred_element_type=F32).reshape(N_CHAN, CH, 128)
        imag = jnp.dot(to_imag, both, preferred_element_type=F32).reshape(N_CHAN, CH, 128)
        mixed[slot] = jnp.concatenate([real, imag], axis=1).astype(BF16)

        @pl.loop(0, N_CHAN - 1)
        def _(step):
            back_copy(unit, slot, chan_peer(step)).start()

        keep_back(unit, slot).start()

    for e, owner in enumerate(EXTRA):

        @pl.when(ci == owner)
        def _():
            mix(1, 16 + e)

    mix(0, ci)

    @pl.loop(0, N_CHAN - 1)
    def _(step):
        peer = chan_peer(step)
        unit_copy(peer, 0, peer, ci).wait_send()

    for e, owner in enumerate(EXTRA):

        @pl.when(ci != owner)
        def _():
            unit_copy(16 + e, 1, owner, ci).wait_send()

    @pl.loop(0, N_CHAN - 1)
    def _(step):
        peer = chan_peer(step)
        back_copy(peer, 0, peer).wait_recv()

    keep_back(ci, 0).wait()
    for e, owner in enumerate(EXTRA):

        @pl.when(ci != owner)
        def _():
            back_copy(16 + e, 1, owner).wait_recv()

        @pl.when(ci == owner)
        def _():
            keep_back(16 + e, 1).wait()

    last = back[UNITS - 1].astype(F32)
    for k in range(MINE):
        out_ref[k] = jnp.concatenate(
            [back[k * 3 + b].astype(F32) for b in range(3)] + [last[:, k : k + 1]], axis=1
        ).astype(BF16)

    @pl.loop(0, N_CHAN - 1)
    def _(step):
        back_copy(ci, 0, chan_peer(step)).wait_send()

    for e, owner in enumerate(EXTRA):

        @pl.when(ci == owner)
        def _():
            @pl.loop(0, N_CHAN - 1)
            def _(step):
                back_copy(16 + e, 1, chan_peer(step)).wait_send()


def body(grid_field, legendre, mix_weight, pair_order):
    any_spec = pl.BlockSpec(memory_space=pl.ANY)
    dma = pltpu.SemaphoreType.DMA
    fixed = [jnp.asarray(c) for c in constants()]
    out = pl.pallas_call(
        kernel,
        out_shape=jax.ShapeDtypeStruct((MINE, 16, SLOTS), BF16),
        in_specs=[any_spec] * 11,
        out_specs=pl.BlockSpec(memory_space=pltpu.VMEM),
        scratch_shapes=[
            pltpu.VMEM((LAT * CH, NLON), BF16),
            pltpu.VMEM((MINE, SLOTS, N_LAT * LAT), BF16),
            pltpu.VMEM((1, PAIRS), jnp.int32),
            pltpu.VMEM((2 * ORDERS, NLON), BF16),
            pltpu.VMEM((N_LAT * ROWS, PAIRS), BF16),
            pltpu.VMEM((N_LAT * ROWS, 128), F32),
            pltpu.VMEM((1024, 1024), BF16),
            pltpu.VMEM((8, CH * ROWS), jnp.int32),
            pltpu.VMEM((2, MINE * 16, CH * ROWS), BF16),
            pltpu.VMEM((MINE * 16, PAIRS), jnp.int32),
            pltpu.VMEM((N_LAT, ROWS, 128), BF16),
            pltpu.VMEM((N_LAT, ROWS, 128), BF16),
            pltpu.VMEM((N_CHAN, 16, 128), BF16),
            pltpu.VMEM((UNITS, 16, 128), BF16),
            pltpu.VMEM((2, N_CHAN, 16, 128), BF16),
            pltpu.VMEM((2, N_CHAN, 16, 128), BF16),
            pltpu.VMEM((UNITS, 16, 128), BF16),
            dma((11,)),
            dma((N_LAT,)),
            dma((N_LAT,)),
            dma((N_CHAN,)),
            dma((N_CHAN,)),
            dma((UNITS,)),
            dma((2, N_CHAN)),
            dma((2, N_CHAN)),
            dma((UNITS,)),
        ],
        compiler_params=pltpu.CompilerParams(
            collective_id=0, has_side_effects=True, vmem_limit_bytes=60 * 1024 * 1024
        ),
    )(
        grid_field.reshape(LAT * CH, NLON),
        jnp.transpose(legendre, (1, 2, 0)),
        mix_weight.reshape(16, 128),
        pair_order.reshape(1, PAIRS),
        *fixed,
    )
    return out.reshape(MINE, 2, CH, SLOTS)


def solution(mesh):
    return jax.shard_map(
        body,
        mesh=mesh,
        in_specs=(P("lat", "chan", None), P(None, "lat", None), P(None, "chan", None), P()),
        out_specs=P("lat", None, "chan", None),
        check_vma=False,
    )
```

```python
import math

import jax
import jax.numpy as jnp
import ml_dtypes
import numpy as np
from jax import lax
from jax.experimental import pallas as pl
from jax.experimental.pallas import tpu as pltpu
from jax.sharding import PartitionSpec as P

BF16 = jnp.bfloat16
F32 = jnp.float32
NX, NY, NZ = 4, 8, 8
N_LAT, N_CHAN = NX * NY, 2 * NZ
LAT, CH, NLON = 16, 8, 1440
ORDERS, SLOTS, PAIRS, MINE = 384, 385, 192, 6
ROWS = 4 * MINE
UNITS = 19
APART = 5
MESH = pl.DeviceIdType.MESH
NT = (((1,), (1,)), ((), ()))


def hops(step, ring):
    return min(step, ring - step)


LAT_STEPS = sorted(
    [(dx, dy) for dx in range(NX) for dy in range(NY) if dx + dy],
    key=lambda d: -hops(d[0], NX) - hops(d[1], NY),
)
CHAN_STEPS = sorted(
    [(dz, dc) for dz in range(NZ) for dc in range(2) if dz + dc],
    key=lambda d: -2 * hops(d[0], NZ) - d[1],
)


def fourier_table():
    orders = np.arange(ORDERS, dtype=np.int32)[:, None]
    columns = np.arange(NLON, dtype=np.int32)[None, :]
    phases = np.float32(2.0 * math.pi / NLON) * ((orders * columns) % NLON).astype(np.float32)
    return np.concatenate([np.cos(phases), -np.sin(phases)], axis=0).astype(ml_dtypes.bfloat16)


def constants():
    row = np.arange(N_LAT * ROWS)
    part, half, pair = (row // 12) % 2, (row // 6) % 2, (row // ROWS) * MINE + row % MINE
    pick = np.zeros((row.size, PAIRS), np.float32)
    pick[row, pair] = 1 - 2 * half
    base = np.broadcast_to((part * ORDERS + half * (ORDERS - 1))[:, None], (row.size, 128))
    s, t, c = np.meshgrid(np.arange(8), np.arange(LAT), np.arange(CH), indexing="ij")
    regroup = np.zeros((1024, 1024), np.float32)
    regroup[(s * 128 + t * CH + c).ravel(), (c * 128 + s * LAT + t).ravel()] = 1
    lane = np.arange(CH * ROWS)
    pair_lane = np.broadcast_to((lane % MINE)[None, :], (8, lane.size))
    k, r, c = np.meshgrid(np.arange(MINE), np.arange(2), np.arange(CH), indexing="ij")
    fold = np.zeros((2, MINE * 16 + 16, CH * ROWS), np.float32)
    for half in range(2):
        fold[half, (k * 16 + r * 8 + c).ravel(), (c * ROWS + r * 12 + half * MINE + k).ravel()] = 1
    out_row = np.arange(MINE * 16)
    offset = np.arange(PAIRS)[None, :] - (out_row // 16)[:, None]
    index = np.concatenate([offset, pair_lane]).astype(np.int32)
    bf = ml_dtypes.bfloat16
    return (
        fourier_table(),
        pick.astype(bf),
        base.astype(np.float32),
        regroup.astype(bf),
        fold.astype(bf),
        index,
    )


def drain(buffer, sem):
    pltpu.make_async_copy(buffer, buffer, sem).wait()


def kernel(
    x_hbm, leg_hbm, mix_hbm, order_hbm, table_hbm, pick_hbm, base_hbm, regroup_hbm, fold_hbm, index_hbm,
    out_ref,
    x, leg, order, table, pick, base, regroup, fold, index,
    send, recv, weights, units, gathered, mixed, back,
    local_sem, lat_send, lat_recv, w_send, w_recv, c_send, c_recv, m_send, m_recv,
):
    li, ci = lax.axis_index("lat"), lax.axis_index("chan")
    loads = [
        pltpu.make_async_copy(src, dst, local_sem.at[i])
        for i, (src, dst) in enumerate(
            [
                (order_hbm, order), (pick_hbm, pick), (base_hbm, base), (x_hbm, x), (table_hbm, table),
                (mix_hbm, weights.at[ci]), (index_hbm, index), (fold_hbm, fold), (regroup_hbm, regroup),
                (leg_hbm, leg),
            ]
        )
    ]
    lx, ly, cz, cc = lax.div(li, NY), lax.rem(li, NY), lax.div(ci, 2), lax.rem(ci, 2)
    xs = [lax.rem(lx + d, NX) * NY for d in range(NX)]
    ys = [lax.rem(ly + d, NY) for d in range(NY)]
    zs = [lax.rem(cz + d, NZ) * 2 for d in range(NZ)]
    cs = [lax.rem(cc + d, 2) for d in range(2)]
    lat_peers = [xs[dx] + ys[dy] for dx, dy in LAT_STEPS]
    chan_peers = [zs[dz] + cs[dc] for dz, dc in CHAN_STEPS]

    barrier = pltpu.get_barrier_semaphore()
    for peer in lat_peers:
        pl.semaphore_signal(barrier, inc=1, device_id=(peer, ci), device_id_type=MESH)
    for peer in chan_peers:
        pl.semaphore_signal(barrier, inc=1, device_id=(li, peer), device_id_type=MESH)
    for load in loads:
        load.start()
    for load in loads[:3]:
        load.wait()
    order_rows = jnp.broadcast_to(order[...], (128, PAIRS)).astype(F32).astype(BF16)
    key = base[...] + lax.dot_general(pick[...], order_rows, NT, preferred_element_type=F32)
    column = lax.broadcasted_iota(jnp.int32, key.shape, 1).astype(F32)
    place = jnp.concatenate(
        [jnp.where(key == column + 128.0 * b, 1.0, 0.0).astype(BF16) for b in range(2 * ORDERS // 128)],
        axis=1,
    )
    for load in loads[3:5]:
        load.wait()
    spectrum = lax.dot_general(table[...], x[...], NT, preferred_element_type=F32)
    spectrum = (spectrum * (1.0 / math.sqrt(NLON))).astype(BF16)
    placed = jnp.dot(place, spectrum, preferred_element_type=F32)
    send[...] = placed.reshape(N_LAT, ROWS, 128).astype(BF16)

    pl.semaphore_wait(barrier, N_LAT + N_CHAN - 2)

    for peer in lat_peers:
        pltpu.make_async_remote_copy(
            src_ref=send.at[peer], dst_ref=recv.at[li], send_sem=lat_send.at[0], recv_sem=lat_recv.at[0],
            device_id=(peer, ci), device_id_type=MESH,
        ).start()
    pltpu.make_async_copy(send.at[li], recv.at[li], lat_recv.at[0]).start()
    loads[5].wait()
    for peer in chan_peers:
        pltpu.make_async_remote_copy(
            src_ref=weights.at[ci], dst_ref=weights.at[ci], send_sem=w_send.at[0], recv_sem=w_recv.at[0],
            device_id=(li, peer), device_id_type=MESH,
        ).start()

    for load in loads[6:]:
        load.wait()
    mine = jnp.where(index[0 : MINE * 16] == li * MINE, 1.0, 0.0).astype(BF16)
    my_order = lax.dot_general(mine, order_rows, NT, preferred_element_type=F32)
    first = lax.broadcasted_iota(jnp.int32, (MINE * 16, SLOTS), 1).astype(F32) < (
        float(ORDERS) - my_order[:, 0:1]
    )

    drain(recv, lat_recv.at[0])
    blocks = jnp.concatenate(
        [
            jnp.concatenate([recv[g * 8 + s].astype(F32) for s in range(8)], axis=1)
            for g in range(N_LAT // 8)
        ],
        axis=0,
    ).astype(BF16)
    turned = jnp.dot(blocks, regroup[...], preferred_element_type=F32)
    fields = jnp.concatenate(
        [
            jnp.concatenate(
                [turned[g * ROWS : (g + 1) * ROWS, c * 128 : (c + 1) * 128] for g in range(N_LAT // 8)],
                axis=1,
            )
            for c in range(CH)
        ],
        axis=0,
    ).astype(BF16)
    lanes = jnp.broadcast_to(index[MINE * 16 : MINE * 16 + 1], (SLOTS, CH * ROWS))
    sums = jnp.zeros((SLOTS, CH * ROWS), F32)
    for k in range(MINE):
        one = lax.dot_general(leg[k], fields, NT, preferred_element_type=F32)
        sums = jnp.where(lanes == k, one, sums)
    sums = sums.astype(BF16)
    halves = [
        lax.dot_general(fold[h, 0 : MINE * 16], sums, NT, preferred_element_type=F32) for h in range(2)
    ]
    coeffs = jnp.where(first, halves[0], halves[1])
    ends = jnp.zeros((16, 128), F32)
    end_lane = lax.broadcasted_iota(jnp.int32, (16, 128), 1)
    for k in range(MINE):
        piece = coeffs[k * 16 : (k + 1) * 16]
        for b in range(3):
            units[k * 3 + b] = piece[:, b * 128 : (b + 1) * 128].astype(BF16)
        ends = jnp.where(end_lane == k, jnp.broadcast_to(piece[:, ORDERS:], (16, 128)), ends)
    units[UNITS - 1] = ends.astype(BF16)

    def extra_copy(e):
        return pltpu.make_async_remote_copy(
            src_ref=units.at[N_CHAN + e], dst_ref=gathered.at[1, ci], send_sem=c_send.at[1 + e],
            recv_sem=c_recv.at[1], device_id=(li, e * APART), device_id_type=MESH,
        )

    def keep_unit(unit, slot):
        return pltpu.make_async_copy(units.at[unit], gathered.at[slot, ci], c_recv.at[slot])

    def send_back(unit, slot):
        for peer in chan_peers:
            pltpu.make_async_remote_copy(
                src_ref=mixed.at[slot, peer], dst_ref=back.at[unit], send_sem=m_send.at[slot],
                recv_sem=m_recv.at[0], device_id=(li, peer), device_id_type=MESH,
            ).start()
        pltpu.make_async_copy(mixed.at[slot, ci], back.at[unit], m_recv.at[0]).start()

    for peer in chan_peers:
        pltpu.make_async_remote_copy(
            src_ref=units.at[peer], dst_ref=gathered.at[0, ci], send_sem=c_send.at[0],
            recv_sem=c_recv.at[0], device_id=(li, peer), device_id_type=MESH,
        ).start()
    for e in range(UNITS - N_CHAN):

        @pl.when(ci != e * APART)
        def _():
            extra_copy(e).start()

        @pl.when(ci == e * APART)
        def _():
            keep_unit(N_CHAN + e, 1).start()

    keep_unit(ci, 0).start()

    drain(weights.at[pl.ds(0, N_CHAN - 1)], w_recv.at[0])
    every = weights[...].astype(F32).reshape(N_CHAN, 2, CH, 128)
    w_real = every[:, 0].reshape(128, 128)
    w_imag = every[:, 1].reshape(128, 128)
    to_real = jnp.concatenate([w_real, -w_imag], axis=1).astype(BF16)
    to_imag = jnp.concatenate([w_imag, w_real], axis=1).astype(BF16)
    drain(send.at[pl.ds(0, N_LAT - 1)], lat_send.at[0])
    drain(weights.at[pl.ds(0, N_CHAN - 1)], w_send.at[0])

    drain(gathered.at[0], c_recv.at[0])
    for e in range(UNITS - N_CHAN):

        @pl.when(ci == e * APART)
        def _():
            drain(gathered.at[1], c_recv.at[1])

    both = gathered[...].astype(F32).reshape(2, N_CHAN, 2, CH, 128)
    both = jnp.concatenate(
        [
            jnp.concatenate([both[slot, :, part].reshape(128, 128) for slot in range(2)], axis=1)
            for part in range(2)
        ],
        axis=0,
    ).astype(BF16)
    real = jnp.dot(to_real, both, preferred_element_type=F32)
    imag = jnp.dot(to_imag, both, preferred_element_type=F32)
    for slot in range(2):
        parts = [
            whole[:, slot * 128 : (slot + 1) * 128].reshape(N_CHAN, CH, 128) for whole in (real, imag)
        ]
        mixed[slot] = jnp.concatenate(parts, axis=1).astype(BF16)

    send_back(ci, 0)
    for e in range(UNITS - N_CHAN):

        @pl.when(ci == e * APART)
        def _():
            send_back(N_CHAN + e, 1)

    drain(units.at[pl.ds(0, N_CHAN - 1)], c_send.at[0])
    for e in range(UNITS - N_CHAN):

        @pl.when(ci != e * APART)
        def _():
            extra_copy(e).wait_send()

    drain(back, m_recv.at[0])
    last = back[UNITS - 1].astype(F32)
    for k in range(MINE):
        out_ref[k] = jnp.concatenate(
            [back[k * 3 + b].astype(F32) for b in range(3)] + [last[:, k : k + 1]], axis=1
        ).astype(BF16)

    drain(mixed.at[0, pl.ds(0, N_CHAN - 1)], m_send.at[0])
    for e in range(UNITS - N_CHAN):

        @pl.when(ci == e * APART)
        def _():
            drain(mixed.at[1, pl.ds(0, N_CHAN - 1)], m_send.at[1])


def body(grid_field, legendre, mix_weight, pair_order):
    any_spec = pl.BlockSpec(memory_space=pl.ANY)
    dma = pltpu.SemaphoreType.DMA
    fixed = [jnp.asarray(c) for c in constants()]
    out = pl.pallas_call(
        kernel,
        out_shape=jax.ShapeDtypeStruct((MINE, 16, SLOTS), BF16),
        in_specs=[any_spec] * 10,
        out_specs=pl.BlockSpec(memory_space=pltpu.VMEM),
        scratch_shapes=[
            pltpu.VMEM((LAT * CH, NLON), BF16),
            pltpu.VMEM((MINE, SLOTS, N_LAT * LAT), BF16),
            pltpu.VMEM((1, PAIRS), jnp.int32),
            pltpu.VMEM((2 * ORDERS, NLON), BF16),
            pltpu.VMEM((N_LAT * ROWS, PAIRS), BF16),
            pltpu.VMEM((N_LAT * ROWS, 128), F32),
            pltpu.VMEM((1024, 1024), BF16),
            pltpu.VMEM((2, MINE * 16 + 16, CH * ROWS), BF16),
            pltpu.VMEM((MINE * 16 + 8, PAIRS), jnp.int32),
            pltpu.VMEM((N_LAT, ROWS, 128), BF16),
            pltpu.VMEM((N_LAT, ROWS, 128), BF16),
            pltpu.VMEM((N_CHAN, 16, 128), BF16),
            pltpu.VMEM((UNITS, 16, 128), BF16),
            pltpu.VMEM((2, N_CHAN, 16, 128), BF16),
            pltpu.VMEM((2, N_CHAN, 16, 128), BF16),
            pltpu.VMEM((UNITS, 16, 128), BF16),
            dma((10,)),
            dma((1,)),
            dma((1,)),
            dma((1,)),
            dma((1,)),
            dma((1 + UNITS - N_CHAN,)),
            dma((2,)),
            dma((2,)),
            dma((1,)),
        ],
        compiler_params=pltpu.CompilerParams(
            collective_id=0, has_side_effects=True, vmem_limit_bytes=60 * 1024 * 1024
        ),
    )(
        grid_field.reshape(LAT * CH, NLON),
        jnp.transpose(legendre, (1, 2, 0)),
        mix_weight.reshape(16, 128),
        pair_order.reshape(1, PAIRS),
        *fixed,
    )
    return out.reshape(MINE, 2, CH, SLOTS)


def solution(mesh):
    return jax.shard_map(
        body,
        mesh=mesh,
        in_specs=(P("lat", "chan", None), P(None, "lat", None), P(None, "chan", None), P()),
        out_specs=P("lat", None, "chan", None),
        check_vma=False,
    )
```

```python
import math

import jax
import jax.numpy as jnp
import ml_dtypes
import numpy as np
from jax import lax
from jax.experimental import pallas as pl
from jax.experimental.pallas import tpu as pltpu
from jax.sharding import PartitionSpec as P

BF16 = jnp.bfloat16
F32 = jnp.float32
NX, NY, NZ = 4, 8, 8
N_LAT, N_CHAN = NX * NY, 2 * NZ
LAT, CH, NLON = 16, 8, 1440
ORDERS, SLOTS, PAIRS, MINE = 384, 385, 192, 6
ROWS = 4 * MINE
UNITS = 19
APART = 5
MESH = pl.DeviceIdType.MESH
NT = (((1,), (1,)), ((), ()))


def hops(step, ring):
    return min(step, ring - step)


LAT_STEPS = sorted(
    [(dx, dy) for dx in range(NX) for dy in range(NY) if dx + dy],
    key=lambda d: -hops(d[0], NX) - hops(d[1], NY),
)
CHAN_STEPS = sorted(
    [(dz, dc) for dz in range(NZ) for dc in range(2) if dz + dc],
    key=lambda d: -2 * hops(d[0], NZ) - d[1],
)


def fourier_table():
    orders = np.arange(ORDERS, dtype=np.int32)[:, None]
    columns = np.arange(NLON, dtype=np.int32)[None, :]
    phases = np.float32(2.0 * math.pi / NLON) * ((orders * columns) % NLON).astype(np.float32)
    return np.concatenate([np.cos(phases), -np.sin(phases)], axis=0).astype(ml_dtypes.bfloat16)


def constants():
    row = np.arange(N_LAT * ROWS)
    part, half, pair = (row // 12) % 2, (row // 6) % 2, (row // ROWS) * MINE + row % MINE
    pick = np.zeros((row.size, PAIRS), np.float32)
    pick[row, pair] = 1 - 2 * half
    base = np.broadcast_to((part * ORDERS + half * (ORDERS - 1))[:, None], (row.size, 128))
    s, t, c = np.meshgrid(np.arange(8), np.arange(LAT), np.arange(CH), indexing="ij")
    regroup = np.zeros((1024, 1024), np.float32)
    regroup[(s * 128 + t * CH + c).ravel(), (c * 128 + s * LAT + t).ravel()] = 1
    lane = np.arange(CH * ROWS)
    pair_lane = np.broadcast_to((lane % MINE)[None, :], (8, lane.size))
    k, r, c = np.meshgrid(np.arange(MINE), np.arange(2), np.arange(CH), indexing="ij")
    fold = np.zeros((2, MINE * 16 + 16, CH * ROWS), np.float32)
    for half in range(2):
        fold[half, (k * 16 + r * 8 + c).ravel(), (c * ROWS + r * 12 + half * MINE + k).ravel()] = 1
    out_row = np.arange(MINE * 16)
    offset = np.arange(PAIRS)[None, :] - (out_row // 16)[:, None]
    index = np.concatenate([offset, pair_lane]).astype(np.int32)
    bf = ml_dtypes.bfloat16
    return (
        fourier_table(),
        pick.astype(bf),
        base.astype(np.float32),
        regroup.astype(bf),
        fold.astype(bf),
        index,
    )


def drain(buffer, sem):
    pltpu.make_async_copy(buffer, buffer, sem).wait()


def kernel(
    x_hbm, leg_hbm, mix_hbm, order_hbm, table_hbm, pick_hbm, base_hbm, regroup_hbm, fold_hbm, index_hbm,
    out_ref,
    x, leg, order, table, pick, base, regroup, fold, index,
    send, recv, weights, units, gathered, mixed, back,
    local_sem, lat_send, lat_recv, w_send, w_recv, c_send, c_recv, m_send, m_recv,
):
    li, ci = lax.axis_index("lat"), lax.axis_index("chan")
    loads = [
        pltpu.make_async_copy(src, dst, local_sem.at[i])
        for i, (src, dst) in enumerate(
            [
                (order_hbm, order), (pick_hbm, pick), (base_hbm, base), (x_hbm, x), (table_hbm, table),
                (mix_hbm, weights.at[ci]), (index_hbm, index), (fold_hbm, fold), (regroup_hbm, regroup),
                (leg_hbm, leg),
            ]
        )
    ]
    lx, ly, cz, cc = lax.div(li, NY), lax.rem(li, NY), lax.div(ci, 2), lax.rem(ci, 2)
    xs = [lax.rem(lx + d, NX) * NY for d in range(NX)]
    ys = [lax.rem(ly + d, NY) for d in range(NY)]
    zs = [lax.rem(cz + d, NZ) * 2 for d in range(NZ)]
    cs = [lax.rem(cc + d, 2) for d in range(2)]
    lat_peers = [xs[dx] + ys[dy] for dx, dy in LAT_STEPS]
    chan_peers = [zs[dz] + cs[dc] for dz, dc in CHAN_STEPS]

    barrier = pltpu.get_barrier_semaphore()
    for peer in lat_peers:
        pl.semaphore_signal(barrier, inc=1, device_id=(peer, ci), device_id_type=MESH)
    for peer in chan_peers:
        pl.semaphore_signal(barrier, inc=1, device_id=(li, peer), device_id_type=MESH)
    for load in loads:
        load.start()
    for load in loads[:3]:
        load.wait()
    order_rows = jnp.broadcast_to(order[...], (128, PAIRS)).astype(F32).astype(BF16)
    key = base[...] + lax.dot_general(pick[...], order_rows, NT, preferred_element_type=F32)
    column = lax.broadcasted_iota(jnp.int32, key.shape, 1).astype(F32)
    place = jnp.concatenate(
        [jnp.where(key == column + 128.0 * b, 1.0, 0.0).astype(BF16) for b in range(2 * ORDERS // 128)],
        axis=1,
    )
    for load in loads[3:5]:
        load.wait()
    spectrum = lax.dot_general(table[...], x[...], NT, preferred_element_type=F32)
    spectrum = (spectrum * (1.0 / math.sqrt(NLON))).astype(BF16)
    placed = jnp.dot(place, spectrum, preferred_element_type=F32)
    send[...] = placed.reshape(N_LAT, ROWS, 128).astype(BF16)

    pl.semaphore_wait(barrier, N_LAT + N_CHAN - 2)

    for peer in lat_peers:
        pltpu.make_async_remote_copy(
            src_ref=send.at[peer], dst_ref=recv.at[li], send_sem=lat_send.at[0], recv_sem=lat_recv.at[0],
            device_id=(peer, ci), device_id_type=MESH,
        ).start()
    pltpu.make_async_copy(send.at[li], recv.at[li], lat_recv.at[0]).start()
    loads[5].wait()
    for peer in chan_peers:
        pltpu.make_async_remote_copy(
            src_ref=weights.at[ci], dst_ref=weights.at[ci], send_sem=w_send.at[0], recv_sem=w_recv.at[0],
            device_id=(li, peer), device_id_type=MESH,
        ).start()

    for load in loads[6:]:
        load.wait()
    mine = jnp.where(index[0 : MINE * 16] == li * MINE, 1.0, 0.0).astype(BF16)
    my_order = lax.dot_general(mine, order_rows, NT, preferred_element_type=F32)
    first = lax.broadcasted_iota(jnp.int32, (MINE * 16, SLOTS), 1).astype(F32) < (
        float(ORDERS) - my_order[:, 0:1]
    )

    drain(recv, lat_recv.at[0])
    blocks = jnp.concatenate(
        [
            jnp.concatenate([recv[g * 8 + s].astype(F32) for s in range(8)], axis=1)
            for g in range(N_LAT // 8)
        ],
        axis=0,
    ).astype(BF16)
    turned = jnp.dot(blocks, regroup[...], preferred_element_type=F32)
    fields = jnp.concatenate(
        [
            jnp.concatenate(
                [turned[g * ROWS : (g + 1) * ROWS, c * 128 : (c + 1) * 128] for g in range(N_LAT // 8)],
                axis=1,
            )
            for c in range(CH)
        ],
        axis=0,
    ).astype(BF16)
    lanes = jnp.broadcast_to(index[MINE * 16 : MINE * 16 + 1], (SLOTS, CH * ROWS))
    sums = jnp.zeros((SLOTS, CH * ROWS), F32)
    for k in range(MINE):
        one = lax.dot_general(leg[k], fields, NT, preferred_element_type=F32)
        sums = jnp.where(lanes == k, one, sums)
    sums = sums.astype(BF16)
    halves = [
        lax.dot_general(fold[h, 0 : MINE * 16], sums, NT, preferred_element_type=F32) for h in range(2)
    ]
    coeffs = jnp.where(first, halves[0], halves[1])
    ends = jnp.zeros((16, 128), F32)
    end_lane = lax.broadcasted_iota(jnp.int32, (16, 128), 1)
    for k in range(MINE):
        piece = coeffs[k * 16 : (k + 1) * 16]
        for b in range(3):
            units[k * 3 + b] = piece[:, b * 128 : (b + 1) * 128].astype(BF16)
        ends = jnp.where(end_lane == k, jnp.broadcast_to(piece[:, ORDERS:], (16, 128)), ends)
    units[UNITS - 1] = ends.astype(BF16)

    def extra_copy(e):
        return pltpu.make_async_remote_copy(
            src_ref=units.at[N_CHAN + e], dst_ref=gathered.at[1, ci], send_sem=c_send.at[1 + e],
            recv_sem=c_recv.at[1], device_id=(li, e * APART), device_id_type=MESH,
        )

    def keep_unit(unit, slot):
        return pltpu.make_async_copy(units.at[unit], gathered.at[slot, ci], c_recv.at[slot])

    def send_back(unit, slot):
        for peer in chan_peers:
            pltpu.make_async_remote_copy(
                src_ref=mixed.at[slot, peer], dst_ref=back.at[unit], send_sem=m_send.at[slot],
                recv_sem=m_recv.at[0], device_id=(li, peer), device_id_type=MESH,
            ).start()
        pltpu.make_async_copy(mixed.at[slot, ci], back.at[unit], m_recv.at[0]).start()

    for peer in chan_peers:
        pltpu.make_async_remote_copy(
            src_ref=units.at[peer], dst_ref=gathered.at[0, ci], send_sem=c_send.at[0],
            recv_sem=c_recv.at[0], device_id=(li, peer), device_id_type=MESH,
        ).start()
    for e in range(UNITS - N_CHAN):

        @pl.when(ci != e * APART)
        def _():
            extra_copy(e).start()

        @pl.when(ci == e * APART)
        def _():
            keep_unit(N_CHAN + e, 1).start()

    keep_unit(ci, 0).start()

    drain(weights.at[pl.ds(0, N_CHAN - 1)], w_recv.at[0])
    every = weights[...].astype(F32).reshape(N_CHAN, 2, CH, 128)
    w_real = every[:, 0].reshape(128, 128)
    w_imag = every[:, 1].reshape(128, 128)
    to_real = jnp.concatenate([w_real, -w_imag], axis=1).astype(BF16)
    to_imag = jnp.concatenate([w_imag, w_real], axis=1).astype(BF16)
    drain(send.at[pl.ds(0, N_LAT - 1)], lat_send.at[0])
    drain(weights.at[pl.ds(0, N_CHAN - 1)], w_send.at[0])

    drain(gathered.at[0], c_recv.at[0])
    for e in range(UNITS - N_CHAN):

        @pl.when(ci == e * APART)
        def _():
            drain(gathered.at[1], c_recv.at[1])

    both = gathered[...].astype(F32).reshape(2, N_CHAN, 2, CH, 128)
    both = jnp.concatenate(
        [
            jnp.concatenate([both[slot, :, part].reshape(128, 128) for slot in range(2)], axis=1)
            for part in range(2)
        ],
        axis=0,
    ).astype(BF16)
    real = jnp.dot(to_real, both, preferred_element_type=F32)
    imag = jnp.dot(to_imag, both, preferred_element_type=F32)
    for slot in range(2):
        parts = [
            whole[:, slot * 128 : (slot + 1) * 128].reshape(N_CHAN, CH, 128) for whole in (real, imag)
        ]
        mixed[slot] = jnp.concatenate(parts, axis=1).astype(BF16)

    send_back(ci, 0)
    for e in range(UNITS - N_CHAN):

        @pl.when(ci == e * APART)
        def _():
            send_back(N_CHAN + e, 1)

    drain(units.at[pl.ds(0, N_CHAN - 1)], c_send.at[0])
    for e in range(UNITS - N_CHAN):

        @pl.when(ci != e * APART)
        def _():
            extra_copy(e).wait_send()

    drain(back, m_recv.at[0])
    last = back[UNITS - 1].astype(F32)
    for k in range(MINE):
        out_ref[k] = jnp.concatenate(
            [back[k * 3 + b].astype(F32) for b in range(3)] + [last[:, k : k + 1]], axis=1
        ).astype(BF16)

    drain(mixed.at[0, pl.ds(0, N_CHAN - 1)], m_send.at[0])
    for e in range(UNITS - N_CHAN):

        @pl.when(ci == e * APART)
        def _():
            drain(mixed.at[1, pl.ds(0, N_CHAN - 1)], m_send.at[1])


def body(grid_field, legendre, mix_weight, pair_order):
    any_spec = pl.BlockSpec(memory_space=pl.ANY)
    dma = pltpu.SemaphoreType.DMA
    fixed = [jnp.asarray(c) for c in constants()]
    out = pl.pallas_call(
        kernel,
        out_shape=pltpu.VMEM((MINE, 16, SLOTS), BF16),
        in_specs=[any_spec] * 10,
        out_specs=pl.BlockSpec(memory_space=pltpu.VMEM),
        scratch_shapes=[
            pltpu.VMEM((LAT * CH, NLON), BF16),
            pltpu.VMEM((MINE, SLOTS, N_LAT * LAT), BF16),
            pltpu.VMEM((1, PAIRS), jnp.int32),
            pltpu.VMEM((2 * ORDERS, NLON), BF16),
            pltpu.VMEM((N_LAT * ROWS, PAIRS), BF16),
            pltpu.VMEM((N_LAT * ROWS, 128), F32),
            pltpu.VMEM((1024, 1024), BF16),
            pltpu.VMEM((2, MINE * 16 + 16, CH * ROWS), BF16),
            pltpu.VMEM((MINE * 16 + 8, PAIRS), jnp.int32),
            pltpu.VMEM((N_LAT, ROWS, 128), BF16),
            pltpu.VMEM((N_LAT, ROWS, 128), BF16),
            pltpu.VMEM((N_CHAN, 16, 128), BF16),
            pltpu.VMEM((UNITS, 16, 128), BF16),
            pltpu.VMEM((2, N_CHAN, 16, 128), BF16),
            pltpu.VMEM((2, N_CHAN, 16, 128), BF16),
            pltpu.VMEM((UNITS, 16, 128), BF16),
            dma((10,)),
            dma((1,)),
            dma((1,)),
            dma((1,)),
            dma((1,)),
            dma((1 + UNITS - N_CHAN,)),
            dma((2,)),
            dma((2,)),
            dma((1,)),
        ],
        compiler_params=pltpu.CompilerParams(
            collective_id=0, has_side_effects=True, vmem_limit_bytes=60 * 1024 * 1024
        ),
    )(
        grid_field.reshape(LAT * CH, NLON),
        jnp.transpose(legendre, (1, 2, 0)),
        mix_weight.reshape(16, 128),
        pair_order.reshape(1, PAIRS),
        *fixed,
    )
    return out.reshape(MINE, 2, CH, SLOTS)


def solution(mesh):
    return jax.shard_map(
        body,
        mesh=mesh,
        in_specs=(P("lat", "chan", None), P(None, "lat", None), P(None, "chan", None), P()),
        out_specs=P("lat", None, "chan", None),
        check_vma=False,
    )
```

```python
import math

import jax
import jax.numpy as jnp
import ml_dtypes
import numpy as np
from jax import lax
from jax.experimental import pallas as pl
from jax.experimental.pallas import tpu as pltpu
from jax.sharding import PartitionSpec as P

BF16 = jnp.bfloat16
F32 = jnp.float32
NX, NY, NZ = 4, 8, 8
N_LAT, N_CHAN = NX * NY, 2 * NZ
LAT, CH, NLON = 16, 8, 1440
ORDERS, SLOTS, PAIRS, MINE = 384, 385, 192, 6
ROWS = 4 * MINE
UNITS = 19
APART = 5
MESH = pl.DeviceIdType.MESH
NT = (((1,), (1,)), ((), ()))


def hops(step, ring):
    return min(step, ring - step)


LAT_STEPS = sorted(
    [(dx, dy) for dx in range(NX) for dy in range(NY) if dx + dy],
    key=lambda d: -hops(d[0], NX) - hops(d[1], NY),
)
CHAN_STEPS = sorted(
    [(dz, dc) for dz in range(NZ) for dc in range(2) if dz + dc],
    key=lambda d: -2 * hops(d[0], NZ) - d[1],
)


def fourier_table():
    orders = np.arange(ORDERS, dtype=np.int32)[:, None]
    columns = np.arange(NLON, dtype=np.int32)[None, :]
    phases = np.float32(2.0 * math.pi / NLON) * ((orders * columns) % NLON).astype(np.float32)
    return np.concatenate([np.cos(phases), -np.sin(phases)], axis=0).astype(ml_dtypes.bfloat16)


def constants():
    row = np.arange(N_LAT * ROWS)
    part, half, pair = (row // 12) % 2, (row // 6) % 2, (row // ROWS) * MINE + row % MINE
    pick = np.zeros((row.size, PAIRS), np.float32)
    pick[row, pair] = 1 - 2 * half
    base = np.broadcast_to((part * ORDERS + half * (ORDERS - 1))[:, None], (row.size, 128))
    s, t, c = np.meshgrid(np.arange(8), np.arange(LAT), np.arange(CH), indexing="ij")
    regroup = np.zeros((1024, 1024), np.float32)
    regroup[(s * 128 + t * CH + c).ravel(), (c * 128 + s * LAT + t).ravel()] = 1
    k, r, c = np.meshgrid(np.arange(MINE), np.arange(2), np.arange(CH), indexing="ij")
    arrange = np.zeros((CH * ROWS, CH * ROWS), np.float32)
    for half in range(2):
        arrange[(k * 32 + half * 16 + r * 8 + c).ravel(), (c * ROWS + r * 12 + half * MINE + k).ravel()] = 1
    out_row = np.arange(MINE * 16)
    offset = np.arange(PAIRS)[None, :] - (out_row // 16)[:, None]
    index = offset.astype(np.int32)
    bf = ml_dtypes.bfloat16
    return (
        fourier_table(),
        pick.astype(bf),
        base.astype(np.float32),
        regroup.astype(bf),
        arrange.astype(bf),
        index,
    )


def drain(buffer, sem):
    pltpu.make_async_copy(buffer, buffer, sem).wait()


def kernel(
    x_hbm, leg_hbm, mix_hbm, order_hbm, table_hbm, pick_hbm, base_hbm, regroup_hbm, arrange_hbm, index_hbm,
    out_ref,
    x, leg, order, table, pick, base, regroup, arrange, index,
    send, recv, weights, units, gathered, mixed, back,
    local_sem, lat_send, lat_recv, w_send, w_recv, c_send, c_recv, m_send, m_recv,
):
    li, ci = lax.axis_index("lat"), lax.axis_index("chan")
    loads = [
        pltpu.make_async_copy(src, dst, local_sem.at[i])
        for i, (src, dst) in enumerate(
            [
                (order_hbm, order), (pick_hbm, pick), (base_hbm, base), (x_hbm, x), (table_hbm.at[pl.ds(0, ORDERS)], table.at[pl.ds(0, ORDERS)]),
                (mix_hbm, weights.at[ci]), (index_hbm, index), (arrange_hbm, arrange), (regroup_hbm, regroup),
                (leg_hbm, leg), (table_hbm.at[pl.ds(ORDERS, ORDERS)], table.at[pl.ds(ORDERS, ORDERS)]),
            ]
        )
    ]
    lx, ly, cz, cc = lax.div(li, NY), lax.rem(li, NY), lax.div(ci, 2), lax.rem(ci, 2)
    xs = [lax.rem(lx + d, NX) * NY for d in range(NX)]
    ys = [lax.rem(ly + d, NY) for d in range(NY)]
    zs = [lax.rem(cz + d, NZ) * 2 for d in range(NZ)]
    cs = [lax.rem(cc + d, 2) for d in range(2)]
    lat_peers = [xs[dx] + ys[dy] for dx, dy in LAT_STEPS]
    chan_peers = [zs[dz] + cs[dc] for dz, dc in CHAN_STEPS]

    for load in loads[:5]:
        load.start()
    barrier = pltpu.get_barrier_semaphore()
    for peer in lat_peers:
        pl.semaphore_signal(barrier, inc=1, device_id=(peer, ci), device_id_type=MESH)
    for peer in chan_peers:
        pl.semaphore_signal(barrier, inc=1, device_id=(li, peer), device_id_type=MESH)
    for load in loads[10:] + loads[5:10]:
        load.start()
    for load in loads[:3]:
        load.wait()
    order_rows = jnp.broadcast_to(order[...], (128, PAIRS)).astype(F32).astype(BF16)
    key = base[...] + lax.dot_general(pick[...], order_rows, NT, preferred_element_type=F32)
    column = lax.broadcasted_iota(jnp.int32, key.shape, 1).astype(F32)
    place = jnp.concatenate(
        [jnp.where(key == column + 128.0 * b, 1.0, 0.0).astype(BF16) for b in range(2 * ORDERS // 128)],
        axis=1,
    )
    loads[3].wait()
    parts = []
    for load, part in ((loads[4], 0), (loads[10], 1)):
        load.wait()
        rows = table[part * ORDERS : (part + 1) * ORDERS]
        spectrum = lax.dot_general(rows, x[...], NT, preferred_element_type=F32)
        parts.append((spectrum * (1.0 / math.sqrt(NLON))).astype(BF16))
    placed = jnp.dot(place, jnp.concatenate(parts, axis=0), preferred_element_type=F32)
    send[...] = placed.reshape(N_LAT, ROWS, 128).astype(BF16)

    pl.semaphore_wait(barrier, N_LAT + N_CHAN - 2)

    for peer in lat_peers:
        pltpu.make_async_remote_copy(
            src_ref=send.at[peer], dst_ref=recv.at[li], send_sem=lat_send.at[0], recv_sem=lat_recv.at[0],
            device_id=(peer, ci), device_id_type=MESH,
        ).start()
    pltpu.make_async_copy(send.at[li], recv.at[li], lat_recv.at[0]).start()
    loads[5].wait()
    for peer in chan_peers:
        pltpu.make_async_remote_copy(
            src_ref=weights.at[ci], dst_ref=weights.at[ci], send_sem=w_send.at[0], recv_sem=w_recv.at[0],
            device_id=(li, peer), device_id_type=MESH,
        ).start()

    for load in loads[6:10]:
        load.wait()
    mine = jnp.where(index[...] == li * MINE, 1.0, 0.0).astype(BF16)
    my_order = lax.dot_general(mine, order_rows, NT, preferred_element_type=F32)
    first = lax.broadcasted_iota(jnp.int32, (MINE * 16, SLOTS), 1).astype(F32) < (
        float(ORDERS) - my_order[:, 0:1]
    )

    drain(recv, lat_recv.at[0])
    blocks = jnp.concatenate(
        [
            jnp.concatenate([recv[g * 8 + s].astype(F32) for s in range(8)], axis=1)
            for g in range(N_LAT // 8)
        ],
        axis=0,
    ).astype(BF16)
    turned = jnp.dot(blocks, regroup[...], preferred_element_type=F32)
    fields = jnp.concatenate(
        [
            jnp.concatenate(
                [turned[g * ROWS : (g + 1) * ROWS, c * 128 : (c + 1) * 128] for g in range(N_LAT // 8)],
                axis=1,
            )
            for c in range(CH)
        ],
        axis=0,
    ).astype(BF16)
    fields = jnp.dot(arrange[...], fields, preferred_element_type=F32).astype(BF16)
    ends = jnp.zeros((16, 128), F32)
    end_lane = lax.broadcasted_iota(jnp.int32, (16, 128), 1)
    for k in range(MINE):
        sums = lax.dot_general(
            fields[k * 32 : (k + 1) * 32], leg[k], NT, preferred_element_type=F32
        )
        piece = jnp.where(first[k * 16 : (k + 1) * 16], sums[0:16], sums[16:32])
        for b in range(3):
            units[k * 3 + b] = piece[:, b * 128 : (b + 1) * 128].astype(BF16)
        ends = jnp.where(end_lane == k, jnp.broadcast_to(piece[:, ORDERS:], (16, 128)), ends)
    units[UNITS - 1] = ends.astype(BF16)

    def extra_copy(e):
        return pltpu.make_async_remote_copy(
            src_ref=units.at[N_CHAN + e], dst_ref=gathered.at[1, ci], send_sem=c_send.at[1 + e],
            recv_sem=c_recv.at[1], device_id=(li, e * APART), device_id_type=MESH,
        )

    def keep_unit(unit, slot):
        return pltpu.make_async_copy(units.at[unit], gathered.at[slot, ci], c_recv.at[slot])

    def send_back(unit, slot):
        for peer in chan_peers:
            pltpu.make_async_remote_copy(
                src_ref=mixed.at[slot, peer], dst_ref=back.at[unit], send_sem=m_send.at[slot],
                recv_sem=m_recv.at[0], device_id=(li, peer), device_id_type=MESH,
            ).start()
        pltpu.make_async_copy(mixed.at[slot, ci], back.at[unit], m_recv.at[0]).start()

    for peer in chan_peers:
        pltpu.make_async_remote_copy(
            src_ref=units.at[peer], dst_ref=gathered.at[0, ci], send_sem=c_send.at[0],
            recv_sem=c_recv.at[0], device_id=(li, peer), device_id_type=MESH,
        ).start()
    for e in range(UNITS - N_CHAN):

        @pl.when(ci != e * APART)
        def _():
            extra_copy(e).start()

        @pl.when(ci == e * APART)
        def _():
            keep_unit(N_CHAN + e, 1).start()

    keep_unit(ci, 0).start()

    drain(weights.at[pl.ds(0, N_CHAN - 1)], w_recv.at[0])
    every = weights[...].astype(F32).reshape(N_CHAN, 2, CH, 128)
    w_real = every[:, 0].reshape(128, 128)
    w_imag = every[:, 1].reshape(128, 128)
    to_real = jnp.concatenate([w_real, -w_imag], axis=1).astype(BF16)
    to_imag = jnp.concatenate([w_imag, w_real], axis=1).astype(BF16)
    drain(send.at[pl.ds(0, N_LAT - 1)], lat_send.at[0])
    drain(weights.at[pl.ds(0, N_CHAN - 1)], w_send.at[0])

    drain(gathered.at[0], c_recv.at[0])
    for e in range(UNITS - N_CHAN):

        @pl.when(ci == e * APART)
        def _():
            drain(gathered.at[1], c_recv.at[1])

    both = gathered[...].astype(F32).reshape(2, N_CHAN, 2, CH, 128)
    both = jnp.concatenate(
        [
            jnp.concatenate([both[slot, :, part].reshape(128, 128) for slot in range(2)], axis=1)
            for part in range(2)
        ],
        axis=0,
    ).astype(BF16)
    real = jnp.dot(to_real, both, preferred_element_type=F32)
    imag = jnp.dot(to_imag, both, preferred_element_type=F32)
    for slot in range(2):
        parts = [
            whole[:, slot * 128 : (slot + 1) * 128].reshape(N_CHAN, CH, 128) for whole in (real, imag)
        ]
        mixed[slot] = jnp.concatenate(parts, axis=1).astype(BF16)

    send_back(ci, 0)
    for e in range(UNITS - N_CHAN):

        @pl.when(ci == e * APART)
        def _():
            send_back(N_CHAN + e, 1)

    drain(units.at[pl.ds(0, N_CHAN - 1)], c_send.at[0])
    for e in range(UNITS - N_CHAN):

        @pl.when(ci != e * APART)
        def _():
            extra_copy(e).wait_send()

    drain(back, m_recv.at[0])
    last = back[UNITS - 1].astype(F32)
    for k in range(MINE):
        out_ref[k] = jnp.concatenate(
            [back[k * 3 + b].astype(F32) for b in range(3)] + [last[:, k : k + 1]], axis=1
        ).astype(BF16)

    drain(mixed.at[0, pl.ds(0, N_CHAN - 1)], m_send.at[0])
    for e in range(UNITS - N_CHAN):

        @pl.when(ci == e * APART)
        def _():
            drain(mixed.at[1, pl.ds(0, N_CHAN - 1)], m_send.at[1])


def body(grid_field, legendre, mix_weight, pair_order):
    any_spec = pl.BlockSpec(memory_space=pl.ANY)
    dma = pltpu.SemaphoreType.DMA
    fixed = [jnp.asarray(c) for c in constants()]
    out = pl.pallas_call(
        kernel,
        out_shape=pltpu.VMEM((MINE, 16, SLOTS), BF16),
        in_specs=[any_spec] * 10,
        out_specs=pl.BlockSpec(memory_space=pltpu.VMEM),
        scratch_shapes=[
            pltpu.VMEM((LAT * CH, NLON), BF16),
            pltpu.VMEM((MINE, SLOTS, N_LAT * LAT), BF16),
            pltpu.VMEM((1, PAIRS), jnp.int32),
            pltpu.VMEM((2 * ORDERS, NLON), BF16),
            pltpu.VMEM((N_LAT * ROWS, PAIRS), BF16),
            pltpu.VMEM((N_LAT * ROWS, 128), F32),
            pltpu.VMEM((1024, 1024), BF16),
            pltpu.VMEM((CH * ROWS, CH * ROWS), BF16),
            pltpu.VMEM((MINE * 16, PAIRS), jnp.int32),
            pltpu.VMEM((N_LAT, ROWS, 128), BF16),
            pltpu.VMEM((N_LAT, ROWS, 128), BF16),
            pltpu.VMEM((N_CHAN, 16, 128), BF16),
            pltpu.VMEM((UNITS, 16, 128), BF16),
            pltpu.VMEM((2, N_CHAN, 16, 128), BF16),
            pltpu.VMEM((2, N_CHAN, 16, 128), BF16),
            pltpu.VMEM((UNITS, 16, 128), BF16),
            dma((11,)),
            dma((1,)),
            dma((1,)),
            dma((1,)),
            dma((1,)),
            dma((1 + UNITS - N_CHAN,)),
            dma((2,)),
            dma((2,)),
            dma((1,)),
        ],
        compiler_params=pltpu.CompilerParams(
            collective_id=0, has_side_effects=True, vmem_limit_bytes=60 * 1024 * 1024
        ),
    )(
        grid_field.reshape(LAT * CH, NLON),
        jnp.transpose(legendre, (1, 2, 0)),
        mix_weight.reshape(16, 128),
        pair_order.reshape(1, PAIRS),
        *fixed,
    )
    return out.reshape(MINE, 2, CH, SLOTS)


def solution(mesh):
    return jax.shard_map(
        body,
        mesh=mesh,
        in_specs=(P("lat", "chan", None), P(None, "lat", None), P(None, "chan", None), P()),
        out_specs=P("lat", None, "chan", None),
        check_vma=False,
    )
```

```python
import math

import jax
import jax.numpy as jnp
import ml_dtypes
import numpy as np
from jax import lax
from jax.experimental import pallas as pl
from jax.experimental.pallas import tpu as pltpu
from jax.sharding import PartitionSpec as P

BF16 = jnp.bfloat16
F32 = jnp.float32
NX, NY, NZ = 4, 8, 8
N_LAT, N_CHAN = NX * NY, 2 * NZ
LAT, CH, NLON = 16, 8, 1440
ORDERS, SLOTS, PAIRS, MINE = 384, 385, 192, 6
ROWS = 4 * MINE
UNITS = 19
APART = 5
MESH = pl.DeviceIdType.MESH
NT = (((1,), (1,)), ((), ()))


def hops(step, ring):
    return min(step, ring - step)


LAT_STEPS = sorted(
    [(dx, dy) for dx in range(NX) for dy in range(NY) if dx + dy],
    key=lambda d: -hops(d[0], NX) - hops(d[1], NY),
)
CHAN_STEPS = sorted(
    [(dz, dc) for dz in range(NZ) for dc in range(2) if dz + dc],
    key=lambda d: -2 * hops(d[0], NZ) - d[1],
)


def fourier_table():
    orders = np.arange(ORDERS, dtype=np.int32)[:, None]
    columns = np.arange(NLON, dtype=np.int32)[None, :]
    phases = np.float32(2.0 * math.pi / NLON) * ((orders * columns) % NLON).astype(np.float32)
    return np.concatenate([np.cos(phases), -np.sin(phases)], axis=0).astype(ml_dtypes.bfloat16)


def constants():
    row = np.arange(N_LAT * ROWS)
    part, half, pair = (row // 12) % 2, (row // 6) % 2, (row // ROWS) * MINE + row % MINE
    pick = np.zeros((row.size, PAIRS), np.float32)
    pick[row, pair] = 1 - 2 * half
    base = np.broadcast_to((part * ORDERS + half * (ORDERS - 1))[:, None], (row.size, 128))
    s, t, c = np.meshgrid(np.arange(8), np.arange(LAT), np.arange(CH), indexing="ij")
    regroup = np.zeros((1024, 1024), np.float32)
    regroup[(s * 128 + t * CH + c).ravel(), (c * 128 + s * LAT + t).ravel()] = 1
    k, r, c = np.meshgrid(np.arange(MINE), np.arange(2), np.arange(CH), indexing="ij")
    arrange = np.zeros((CH * ROWS, CH * ROWS), np.float32)
    for half in range(2):
        arrange[(k * 32 + half * 16 + r * 8 + c).ravel(), (c * ROWS + r * 12 + half * MINE + k).ravel()] = 1
    out_row = np.arange(MINE * 16)
    offset = np.arange(PAIRS)[None, :] - (out_row // 16)[:, None]
    index = offset.astype(np.int32)
    bf = ml_dtypes.bfloat16
    return (
        fourier_table(),
        pick.astype(bf),
        base.astype(np.float32),
        regroup.astype(bf),
        arrange.astype(bf),
        index,
    )


def drain(buffer, sem):
    pltpu.make_async_copy(buffer, buffer, sem).wait()


def kernel(
    x_hbm, leg_hbm, mix_hbm, order_hbm, table_hbm, pick_hbm, base_hbm, regroup_hbm, arrange_hbm, index_hbm,
    out_ref,
    x, leg, turned_leg, order, table, pick, base, regroup, arrange, index,
    send, recv, weights, units, gathered, mixed, back,
    local_sem, lat_send, lat_recv, w_send, w_recv, c_send, c_recv, m_send, m_recv,
):
    li, ci = lax.axis_index("lat"), lax.axis_index("chan")
    loads = [
        pltpu.make_async_copy(src, dst, local_sem.at[i])
        for i, (src, dst) in enumerate(
            [
                (order_hbm, order), (pick_hbm, pick), (base_hbm, base), (x_hbm, x), (table_hbm.at[pl.ds(0, ORDERS)], table.at[pl.ds(0, ORDERS)]),
                (mix_hbm, weights.at[ci]), (index_hbm, index), (arrange_hbm, arrange), (regroup_hbm, regroup),
                (leg_hbm, leg), (table_hbm.at[pl.ds(ORDERS, ORDERS)], table.at[pl.ds(ORDERS, ORDERS)]),
            ]
        )
    ]
    lx, ly, cz, cc = lax.div(li, NY), lax.rem(li, NY), lax.div(ci, 2), lax.rem(ci, 2)
    xs = [lax.rem(lx + d, NX) * NY for d in range(NX)]
    ys = [lax.rem(ly + d, NY) for d in range(NY)]
    zs = [lax.rem(cz + d, NZ) * 2 for d in range(NZ)]
    cs = [lax.rem(cc + d, 2) for d in range(2)]
    lat_peers = [xs[dx] + ys[dy] for dx, dy in LAT_STEPS]
    chan_peers = [zs[dz] + cs[dc] for dz, dc in CHAN_STEPS]

    for load in loads[:5]:
        load.start()
    barrier = pltpu.get_barrier_semaphore()
    far = [(hops(dx, NX) + hops(dy, NY), peer, ci) for (dx, dy), peer in zip(LAT_STEPS, lat_peers)]
    far += [(hops(dz, NZ), li, peer) for (dz, dc), peer in zip(CHAN_STEPS, chan_peers)]
    for _, lat, chan in sorted(far, key=lambda f: -f[0]):
        pl.semaphore_signal(barrier, inc=1, device_id=(lat, chan), device_id_type=MESH)
    for load in loads[10:] + loads[5:10]:
        load.start()
    for load in loads[:3]:
        load.wait()
    order_rows = jnp.broadcast_to(order[...], (128, PAIRS)).astype(F32).astype(BF16)
    key = base[...] + lax.dot_general(pick[...], order_rows, NT, preferred_element_type=F32)
    column = lax.broadcasted_iota(jnp.int32, key.shape, 1).astype(F32)
    place = jnp.concatenate(
        [jnp.where(key == column + 128.0 * b, 1.0, 0.0).astype(BF16) for b in range(2 * ORDERS // 128)],
        axis=1,
    )
    loads[3].wait()
    parts = []
    for load, part in ((loads[4], 0), (loads[10], 1)):
        load.wait()
        rows = table[part * ORDERS : (part + 1) * ORDERS]
        spectrum = lax.dot_general(rows, x[...], NT, preferred_element_type=F32)
        parts.append((spectrum * (1.0 / math.sqrt(NLON))).astype(BF16))
    placed = jnp.dot(place, jnp.concatenate(parts, axis=0), preferred_element_type=F32)
    send[...] = placed.reshape(N_LAT, ROWS, 128).astype(BF16)

    pl.semaphore_wait(barrier, N_LAT + N_CHAN - 2)

    for peer in lat_peers:
        pltpu.make_async_remote_copy(
            src_ref=send.at[peer], dst_ref=recv.at[li], send_sem=lat_send.at[0], recv_sem=lat_recv.at[0],
            device_id=(peer, ci), device_id_type=MESH,
        ).start()
    pltpu.make_async_copy(send.at[li], recv.at[li], lat_recv.at[0]).start()
    loads[5].wait()
    for peer in chan_peers:
        pltpu.make_async_remote_copy(
            src_ref=weights.at[ci], dst_ref=weights.at[ci], send_sem=w_send.at[0], recv_sem=w_recv.at[0],
            device_id=(li, peer), device_id_type=MESH,
        ).start()

    for load in loads[6:10]:
        load.wait()
    mine = jnp.where(index[...] == li * MINE, 1.0, 0.0).astype(BF16)
    my_order = lax.dot_general(mine, order_rows, NT, preferred_element_type=F32)
    first = lax.broadcasted_iota(jnp.int32, (MINE * 16, SLOTS), 1).astype(F32) < (
        float(ORDERS) - my_order[:, 0:1]
    )

    lat_ids = [lax.broadcasted_iota(jnp.int32, (N_LAT * LAT, N_LAT * LAT), d) for d in range(2)]
    unit = jnp.where(lat_ids[0] == lat_ids[1], 1.0, 0.0).astype(BF16)
    for k in range(MINE):
        turned_leg[k] = lax.dot_general(unit, leg[k], NT, preferred_element_type=F32).astype(BF16)

    drain(recv, lat_recv.at[0])
    blocks = jnp.concatenate(
        [
            jnp.concatenate([recv[g * 8 + s].astype(F32) for s in range(8)], axis=1)
            for g in range(N_LAT // 8)
        ],
        axis=0,
    ).astype(BF16)
    turned = jnp.dot(blocks, regroup[...], preferred_element_type=F32)
    fields = jnp.concatenate(
        [
            jnp.concatenate(
                [turned[g * ROWS : (g + 1) * ROWS, c * 128 : (c + 1) * 128] for g in range(N_LAT // 8)],
                axis=1,
            )
            for c in range(CH)
        ],
        axis=0,
    ).astype(BF16)
    fields = jnp.dot(arrange[...], fields, preferred_element_type=F32).astype(BF16)
    ends = jnp.zeros((16, 128), F32)
    end_lane = lax.broadcasted_iota(jnp.int32, (16, 128), 1)
    for k in range(MINE):
        sums = jnp.dot(fields[k * 32 : (k + 1) * 32], turned_leg[k], preferred_element_type=F32)
        piece = jnp.where(first[k * 16 : (k + 1) * 16], sums[0:16], sums[16:32])
        for b in range(3):
            units[k * 3 + b] = piece[:, b * 128 : (b + 1) * 128].astype(BF16)
        ends = jnp.where(end_lane == k, jnp.broadcast_to(piece[:, ORDERS:], (16, 128)), ends)
    units[UNITS - 1] = ends.astype(BF16)

    def extra_copy(e):
        return pltpu.make_async_remote_copy(
            src_ref=units.at[N_CHAN + e], dst_ref=gathered.at[1, ci], send_sem=c_send.at[1 + e],
            recv_sem=c_recv.at[1], device_id=(li, e * APART), device_id_type=MESH,
        )

    def keep_unit(unit, slot):
        return pltpu.make_async_copy(units.at[unit], gathered.at[slot, ci], c_recv.at[slot])

    def send_back(unit, slot):
        for peer in chan_peers:
            pltpu.make_async_remote_copy(
                src_ref=mixed.at[slot, peer], dst_ref=back.at[unit], send_sem=m_send.at[slot],
                recv_sem=m_recv.at[0], device_id=(li, peer), device_id_type=MESH,
            ).start()
        pltpu.make_async_copy(mixed.at[slot, ci], back.at[unit], m_recv.at[0]).start()

    for peer in chan_peers:
        pltpu.make_async_remote_copy(
            src_ref=units.at[peer], dst_ref=gathered.at[0, ci], send_sem=c_send.at[0],
            recv_sem=c_recv.at[0], device_id=(li, peer), device_id_type=MESH,
        ).start()
    for e in range(UNITS - N_CHAN):

        @pl.when(ci != e * APART)
        def _():
            extra_copy(e).start()

        @pl.when(ci == e * APART)
        def _():
            keep_unit(N_CHAN + e, 1).start()

    keep_unit(ci, 0).start()

    drain(weights.at[pl.ds(0, N_CHAN - 1)], w_recv.at[0])
    every = weights[...].astype(F32).reshape(N_CHAN, 2, CH, 128)
    w_real = every[:, 0].reshape(128, 128)
    w_imag = every[:, 1].reshape(128, 128)
    to_real = jnp.concatenate([w_real, -w_imag], axis=1).astype(BF16)
    to_imag = jnp.concatenate([w_imag, w_real], axis=1).astype(BF16)
    drain(send.at[pl.ds(0, N_LAT - 1)], lat_send.at[0])
    drain(weights.at[pl.ds(0, N_CHAN - 1)], w_send.at[0])

    drain(gathered.at[0], c_recv.at[0])
    for e in range(UNITS - N_CHAN):

        @pl.when(ci == e * APART)
        def _():
            drain(gathered.at[1], c_recv.at[1])

    both = gathered[...].astype(F32).reshape(2, N_CHAN, 2, CH, 128)
    both = jnp.concatenate(
        [
            jnp.concatenate([both[slot, :, part].reshape(128, 128) for slot in range(2)], axis=1)
            for part in range(2)
        ],
        axis=0,
    ).astype(BF16)
    real = jnp.dot(to_real, both, preferred_element_type=F32)
    imag = jnp.dot(to_imag, both, preferred_element_type=F32)
    for slot in range(2):
        parts = [
            whole[:, slot * 128 : (slot + 1) * 128].reshape(N_CHAN, CH, 128) for whole in (real, imag)
        ]
        mixed[slot] = jnp.concatenate(parts, axis=1).astype(BF16)

    send_back(ci, 0)
    for e in range(UNITS - N_CHAN):

        @pl.when(ci == e * APART)
        def _():
            send_back(N_CHAN + e, 1)

    drain(units.at[pl.ds(0, N_CHAN - 1)], c_send.at[0])
    for e in range(UNITS - N_CHAN):

        @pl.when(ci != e * APART)
        def _():
            extra_copy(e).wait_send()

    drain(back, m_recv.at[0])
    last = back[UNITS - 1].astype(F32)
    for k in range(MINE):
        out_ref[k] = jnp.concatenate(
            [back[k * 3 + b].astype(F32) for b in range(3)] + [last[:, k : k + 1]], axis=1
        ).astype(BF16)

    drain(mixed.at[0, pl.ds(0, N_CHAN - 1)], m_send.at[0])
    for e in range(UNITS - N_CHAN):

        @pl.when(ci == e * APART)
        def _():
            drain(mixed.at[1, pl.ds(0, N_CHAN - 1)], m_send.at[1])


def body(grid_field, legendre, mix_weight, pair_order):
    any_spec = pl.BlockSpec(memory_space=pl.ANY)
    dma = pltpu.SemaphoreType.DMA
    fixed = [jnp.asarray(c) for c in constants()]
    out = pl.pallas_call(
        kernel,
        out_shape=pltpu.VMEM((MINE, 16, SLOTS), BF16),
        in_specs=[any_spec] * 10,
        out_specs=pl.BlockSpec(memory_space=pltpu.VMEM),
        scratch_shapes=[
            pltpu.VMEM((LAT * CH, NLON), BF16),
            pltpu.VMEM((MINE, SLOTS, N_LAT * LAT), BF16),
            pltpu.VMEM((MINE, N_LAT * LAT, SLOTS), BF16),
            pltpu.VMEM((1, PAIRS), jnp.int32),
            pltpu.VMEM((2 * ORDERS, NLON), BF16),
            pltpu.VMEM((N_LAT * ROWS, PAIRS), BF16),
            pltpu.VMEM((N_LAT * ROWS, 128), F32),
            pltpu.VMEM((1024, 1024), BF16),
            pltpu.VMEM((CH * ROWS, CH * ROWS), BF16),
            pltpu.VMEM((MINE * 16, PAIRS), jnp.int32),
            pltpu.VMEM((N_LAT, ROWS, 128), BF16),
            pltpu.VMEM((N_LAT, ROWS, 128), BF16),
            pltpu.VMEM((N_CHAN, 16, 128), BF16),
            pltpu.VMEM((UNITS, 16, 128), BF16),
            pltpu.VMEM((2, N_CHAN, 16, 128), BF16),
            pltpu.VMEM((2, N_CHAN, 16, 128), BF16),
            pltpu.VMEM((UNITS, 16, 128), BF16),
            dma((11,)),
            dma((1,)),
            dma((1,)),
            dma((1,)),
            dma((1,)),
            dma((1 + UNITS - N_CHAN,)),
            dma((2,)),
            dma((2,)),
            dma((1,)),
        ],
        compiler_params=pltpu.CompilerParams(
            collective_id=0, has_side_effects=True, vmem_limit_bytes=60 * 1024 * 1024
        ),
    )(
        grid_field.reshape(LAT * CH, NLON),
        jnp.transpose(legendre, (1, 2, 0)),
        mix_weight.reshape(16, 128),
        pair_order.reshape(1, PAIRS),
        *fixed,
    )
    return out.reshape(MINE, 2, CH, SLOTS)


def solution(mesh):
    return jax.shard_map(
        body,
        mesh=mesh,
        in_specs=(P("lat", "chan", None), P(None, "lat", None), P(None, "chan", None), P()),
        out_specs=P("lat", None, "chan", None),
        check_vma=False,
    )
```

```python
import math

import jax
import jax.numpy as jnp
import ml_dtypes
import numpy as np
from jax import lax
from jax.experimental import pallas as pl
from jax.experimental.pallas import tpu as pltpu
from jax.sharding import PartitionSpec as P

BF16 = jnp.bfloat16
F32 = jnp.float32
NX, NY, NZ = 4, 8, 8
N_LAT, N_CHAN = NX * NY, 2 * NZ
LAT, CH, NLON = 16, 8, 1440
ORDERS, SLOTS, PAIRS, MINE = 384, 385, 192, 6
ROWS = 4 * MINE
UNITS = 19
APART = 5
MESH = pl.DeviceIdType.MESH
NT = (((1,), (1,)), ((), ()))


def hops(step, ring):
    return min(step, ring - step)


LAT_STEPS = sorted(
    [(dx, dy) for dx in range(NX) for dy in range(NY) if dx + dy],
    key=lambda d: -hops(d[0], NX) - hops(d[1], NY),
)
CHAN_STEPS = sorted(
    [(dz, dc) for dz in range(NZ) for dc in range(2) if dz + dc],
    key=lambda d: -2 * hops(d[0], NZ) - d[1],
)


def fourier_table():
    orders = np.arange(ORDERS, dtype=np.int32)[:, None]
    columns = np.arange(NLON, dtype=np.int32)[None, :]
    phases = np.float32(2.0 * math.pi / NLON) * ((orders * columns) % NLON).astype(np.float32)
    return np.concatenate([np.cos(phases), -np.sin(phases)], axis=0).astype(ml_dtypes.bfloat16)


def constants():
    row = np.arange(N_LAT * ROWS)
    part, half, pair = (row // 12) % 2, (row // 6) % 2, (row // ROWS) * MINE + row % MINE
    pick = np.zeros((row.size, PAIRS), np.float32)
    pick[row, pair] = 1 - 2 * half
    base = np.broadcast_to((part * ORDERS + half * (ORDERS - 1))[:, None], (row.size, 128))
    s, t, c = np.meshgrid(np.arange(8), np.arange(LAT), np.arange(CH), indexing="ij")
    regroup = np.zeros((1024, 1024), np.float32)
    regroup[(s * 128 + t * CH + c).ravel(), (c * 128 + s * LAT + t).ravel()] = 1
    k, r, c = np.meshgrid(np.arange(MINE), np.arange(2), np.arange(CH), indexing="ij")
    arrange = np.zeros((CH * ROWS, CH * ROWS), np.float32)
    for half in range(2):
        arrange[(k * 32 + half * 16 + r * 8 + c).ravel(), (c * ROWS + r * 12 + half * MINE + k).ravel()] = 1
    out_row = np.arange(MINE * 16)
    offset = np.arange(PAIRS)[None, :] - (out_row // 16)[:, None]
    index = offset.astype(np.int32)
    bf = ml_dtypes.bfloat16
    return (
        fourier_table(),
        pick.astype(bf),
        base.astype(np.float32),
        regroup.astype(bf),
        arrange.astype(bf),
        index,
    )


def drain(buffer, sem):
    pltpu.make_async_copy(buffer, buffer, sem).wait()


def kernel(
    x_hbm, leg_hbm, mix_hbm, order_hbm, table_hbm, pick_hbm, base_hbm, regroup_hbm, arrange_hbm, index_hbm,
    out_ref,
    x, leg, turned_leg, order, table, pick, base, regroup, arrange, index,
    send, recv, weights, units, gathered, mixed, back,
    local_sem, lat_send, lat_recv, w_send, w_recv, c_send, c_recv, m_send, m_recv,
):
    li, ci = lax.axis_index("lat"), lax.axis_index("chan")
    loads = [
        pltpu.make_async_copy(src, dst, local_sem.at[i])
        for i, (src, dst) in enumerate(
            [
                (order_hbm, order), (pick_hbm, pick), (base_hbm, base), (x_hbm, x), (table_hbm.at[pl.ds(0, ORDERS)], table.at[pl.ds(0, ORDERS)]),
                (mix_hbm, weights.at[ci]), (index_hbm, index), (arrange_hbm, arrange), (regroup_hbm, regroup),
                (leg_hbm, leg), (table_hbm.at[pl.ds(ORDERS, ORDERS)], table.at[pl.ds(ORDERS, ORDERS)]),
            ]
        )
    ]
    lx, ly, cz, cc = lax.div(li, NY), lax.rem(li, NY), lax.div(ci, 2), lax.rem(ci, 2)
    xs = [lax.rem(lx + d, NX) * NY for d in range(NX)]
    ys = [lax.rem(ly + d, NY) for d in range(NY)]
    zs = [lax.rem(cz + d, NZ) * 2 for d in range(NZ)]
    cs = [lax.rem(cc + d, 2) for d in range(2)]
    lat_peers = [xs[dx] + ys[dy] for dx, dy in LAT_STEPS]
    chan_peers = [zs[dz] + cs[dc] for dz, dc in CHAN_STEPS]

    for load in loads[:5]:
        load.start()
    barrier = pltpu.get_barrier_semaphore()
    far = [(hops(dx, NX) + hops(dy, NY), peer, ci) for (dx, dy), peer in zip(LAT_STEPS, lat_peers)]
    far += [(hops(dz, NZ), li, peer) for (dz, dc), peer in zip(CHAN_STEPS, chan_peers)]
    for _, lat, chan in sorted(far, key=lambda f: -f[0]):
        pl.semaphore_signal(barrier, inc=1, device_id=(lat, chan), device_id_type=MESH)
    for load in loads[10:] + loads[5:10]:
        load.start()
    for load in loads[:3]:
        load.wait()
    order_rows = jnp.broadcast_to(order[...], (128, PAIRS)).astype(F32).astype(BF16)
    key = base[...] + lax.dot_general(pick[...], order_rows, NT, preferred_element_type=F32)
    column = lax.broadcasted_iota(jnp.int32, key.shape, 1).astype(F32)
    place = jnp.concatenate(
        [jnp.where(key == column + 128.0 * b, 1.0, 0.0).astype(BF16) for b in range(2 * ORDERS // 128)],
        axis=1,
    )
    loads[3].wait()
    parts = []
    for load, part in ((loads[4], 0), (loads[10], 1)):
        load.wait()
        rows = table[part * ORDERS : (part + 1) * ORDERS]
        spectrum = lax.dot_general(rows, x[...], NT, preferred_element_type=F32)
        parts.append((spectrum * (1.0 / math.sqrt(NLON))).astype(BF16))
    placed = jnp.dot(place, jnp.concatenate(parts, axis=0), preferred_element_type=F32)
    send[...] = placed.reshape(N_LAT, ROWS, 128).astype(BF16)

    pl.semaphore_wait(barrier, N_LAT + N_CHAN - 2)

    for peer in lat_peers:
        pltpu.make_async_remote_copy(
            src_ref=send.at[peer], dst_ref=recv.at[li], send_sem=lat_send.at[0], recv_sem=lat_recv.at[0],
            device_id=(peer, ci), device_id_type=MESH,
        ).start()
    pltpu.make_async_copy(send.at[li], recv.at[li], lat_recv.at[0]).start()
    loads[5].wait()
    for peer in chan_peers:
        pltpu.make_async_remote_copy(
            src_ref=weights.at[ci], dst_ref=weights.at[ci], send_sem=w_send.at[0], recv_sem=w_recv.at[0],
            device_id=(li, peer), device_id_type=MESH,
        ).start()

    for load in loads[6:10]:
        load.wait()
    mine = jnp.where(index[...] == li * MINE, 1.0, 0.0).astype(BF16)
    my_order = lax.dot_general(mine, order_rows, NT, preferred_element_type=F32)
    first = lax.broadcasted_iota(jnp.int32, (MINE * 16, SLOTS), 1).astype(F32) < (
        float(ORDERS) - my_order[:, 0:1]
    )

    lat_ids = [lax.broadcasted_iota(jnp.int32, (N_LAT * LAT, N_LAT * LAT), d) for d in range(2)]
    unit = jnp.where(lat_ids[0] == lat_ids[1], 1.0, 0.0).astype(BF16)
    for k in range(MINE):
        turned_leg[k] = lax.dot_general(unit, leg[k], NT, preferred_element_type=F32).astype(BF16)

    drain(recv, lat_recv.at[0])
    blocks = jnp.concatenate(
        [
            jnp.concatenate([recv[g * 8 + s].astype(F32) for s in range(8)], axis=1)
            for g in range(N_LAT // 8)
        ],
        axis=0,
    ).astype(BF16)
    turned = jnp.dot(blocks, regroup[...], preferred_element_type=F32)
    fields = jnp.concatenate(
        [
            jnp.concatenate(
                [turned[g * ROWS : (g + 1) * ROWS, c * 128 : (c + 1) * 128] for g in range(N_LAT // 8)],
                axis=1,
            )
            for c in range(CH)
        ],
        axis=0,
    ).astype(BF16)
    fields = jnp.dot(arrange[...], fields, preferred_element_type=F32).astype(BF16)
    ends = jnp.zeros((16, 128), F32)
    end_lane = lax.broadcasted_iota(jnp.int32, (16, 128), 1)
    for k in range(MINE):
        sums = jnp.dot(fields[k * 32 : (k + 1) * 32], turned_leg[k], preferred_element_type=F32)
        piece = jnp.where(first[k * 16 : (k + 1) * 16], sums[0:16], sums[16:32])
        for b in range(3):
            units[k * 3 + b] = piece[:, b * 128 : (b + 1) * 128].astype(BF16)
        ends = jnp.where(end_lane == k, jnp.broadcast_to(piece[:, ORDERS:], (16, 128)), ends)
    units[UNITS - 1] = ends.astype(BF16)

    def extra_copy(e):
        return pltpu.make_async_remote_copy(
            src_ref=units.at[N_CHAN + e], dst_ref=gathered.at[1, ci], send_sem=c_send.at[1 + e],
            recv_sem=c_recv.at[1], device_id=(li, e * APART), device_id_type=MESH,
        )

    def keep_unit(unit, slot):
        return pltpu.make_async_copy(units.at[unit], gathered.at[slot, ci], c_recv.at[slot])

    def send_back(unit, slot):
        for peer in chan_peers:
            pltpu.make_async_remote_copy(
                src_ref=mixed.at[slot, peer], dst_ref=back.at[unit], send_sem=m_send.at[slot],
                recv_sem=m_recv.at[0], device_id=(li, peer), device_id_type=MESH,
            ).start()
        pltpu.make_async_copy(mixed.at[slot, ci], back.at[unit], m_recv.at[0]).start()

    for e in range(UNITS - N_CHAN):

        @pl.when(ci != e * APART)
        def _():
            extra_copy(e).start()

        @pl.when(ci == e * APART)
        def _():
            keep_unit(N_CHAN + e, 1).start()

    for peer in chan_peers:
        pltpu.make_async_remote_copy(
            src_ref=units.at[peer], dst_ref=gathered.at[0, ci], send_sem=c_send.at[0],
            recv_sem=c_recv.at[0], device_id=(li, peer), device_id_type=MESH,
        ).start()
    keep_unit(ci, 0).start()

    drain(weights.at[pl.ds(0, N_CHAN - 1)], w_recv.at[0])
    every = weights[...].astype(F32).reshape(N_CHAN, 2, CH, 128)
    w_real = every[:, 0].reshape(128, 128)
    w_imag = every[:, 1].reshape(128, 128)
    to_real = jnp.concatenate([w_real, -w_imag], axis=1).astype(BF16)
    to_imag = jnp.concatenate([w_imag, w_real], axis=1).astype(BF16)
    drain(send.at[pl.ds(0, N_LAT - 1)], lat_send.at[0])
    drain(weights.at[pl.ds(0, N_CHAN - 1)], w_send.at[0])

    drain(gathered.at[0], c_recv.at[0])
    for e in range(UNITS - N_CHAN):

        @pl.when(ci == e * APART)
        def _():
            drain(gathered.at[1], c_recv.at[1])

    both = gathered[...].astype(F32).reshape(2, N_CHAN, 2, CH, 128)
    both = jnp.concatenate(
        [
            jnp.concatenate([both[slot, :, part].reshape(128, 128) for slot in range(2)], axis=1)
            for part in range(2)
        ],
        axis=0,
    ).astype(BF16)
    real = jnp.dot(to_real, both, preferred_element_type=F32)
    imag = jnp.dot(to_imag, both, preferred_element_type=F32)
    for slot in range(2):
        parts = [
            whole[:, slot * 128 : (slot + 1) * 128].reshape(N_CHAN, CH, 128) for whole in (real, imag)
        ]
        mixed[slot] = jnp.concatenate(parts, axis=1).astype(BF16)

    send_back(ci, 0)
    for e in range(UNITS - N_CHAN):

        @pl.when(ci == e * APART)
        def _():
            send_back(N_CHAN + e, 1)

    drain(units.at[pl.ds(0, N_CHAN - 1)], c_send.at[0])
    for e in range(UNITS - N_CHAN):

        @pl.when(ci != e * APART)
        def _():
            extra_copy(e).wait_send()

    drain(back, m_recv.at[0])
    last = back[UNITS - 1].astype(F32)
    for k in range(MINE):
        out_ref[k] = jnp.concatenate(
            [back[k * 3 + b].astype(F32) for b in range(3)] + [last[:, k : k + 1]], axis=1
        ).astype(BF16)

    drain(mixed.at[0, pl.ds(0, N_CHAN - 1)], m_send.at[0])
    for e in range(UNITS - N_CHAN):

        @pl.when(ci == e * APART)
        def _():
            drain(mixed.at[1, pl.ds(0, N_CHAN - 1)], m_send.at[1])


def body(grid_field, legendre, mix_weight, pair_order):
    any_spec = pl.BlockSpec(memory_space=pl.ANY)
    dma = pltpu.SemaphoreType.DMA
    fixed = [jnp.asarray(c) for c in constants()]
    out = pl.pallas_call(
        kernel,
        out_shape=pltpu.VMEM((MINE, 16, SLOTS), BF16),
        in_specs=[any_spec] * 10,
        out_specs=pl.BlockSpec(memory_space=pltpu.VMEM),
        scratch_shapes=[
            pltpu.VMEM((LAT * CH, NLON), BF16),
            pltpu.VMEM((MINE, SLOTS, N_LAT * LAT), BF16),
            pltpu.VMEM((MINE, N_LAT * LAT, SLOTS), BF16),
            pltpu.VMEM((1, PAIRS), jnp.int32),
            pltpu.VMEM((2 * ORDERS, NLON), BF16),
            pltpu.VMEM((N_LAT * ROWS, PAIRS), BF16),
            pltpu.VMEM((N_LAT * ROWS, 128), F32),
            pltpu.VMEM((1024, 1024), BF16),
            pltpu.VMEM((CH * ROWS, CH * ROWS), BF16),
            pltpu.VMEM((MINE * 16, PAIRS), jnp.int32),
            pltpu.VMEM((N_LAT, ROWS, 128), BF16),
            pltpu.VMEM((N_LAT, ROWS, 128), BF16),
            pltpu.VMEM((N_CHAN, 16, 128), BF16),
            pltpu.VMEM((UNITS, 16, 128), BF16),
            pltpu.VMEM((2, N_CHAN, 16, 128), BF16),
            pltpu.VMEM((2, N_CHAN, 16, 128), BF16),
            pltpu.VMEM((UNITS, 16, 128), BF16),
            dma((11,)),
            dma((1,)),
            dma((1,)),
            dma((1,)),
            dma((1,)),
            dma((1 + UNITS - N_CHAN,)),
            dma((2,)),
            dma((2,)),
            dma((1,)),
        ],
        compiler_params=pltpu.CompilerParams(
            collective_id=0, has_side_effects=True, vmem_limit_bytes=60 * 1024 * 1024
        ),
    )(
        grid_field.reshape(LAT * CH, NLON),
        jnp.transpose(legendre, (1, 2, 0)),
        mix_weight.reshape(16, 128),
        pair_order.reshape(1, PAIRS),
        *fixed,
    )
    return out.reshape(MINE, 2, CH, SLOTS)


def solution(mesh):
    return jax.shard_map(
        body,
        mesh=mesh,
        in_specs=(P("lat", "chan", None), P(None, "lat", None), P(None, "chan", None), P()),
        out_specs=P("lat", None, "chan", None),
        check_vma=False,
    )
```

```python
import math

import jax
import jax.numpy as jnp
import ml_dtypes
import numpy as np
from jax import lax
from jax.experimental import pallas as pl
from jax.experimental.pallas import tpu as pltpu
from jax.sharding import PartitionSpec as P

BF16 = jnp.bfloat16
F32 = jnp.float32
NX, NY, NZ = 4, 8, 8
N_LAT, N_CHAN = NX * NY, 2 * NZ
LAT, CH, NLON = 16, 8, 1440
ORDERS, SLOTS, PAIRS, MINE = 384, 385, 192, 6
ROWS = 4 * MINE
UNITS = 19
APART = 5
MESH = pl.DeviceIdType.MESH
NT = (((1,), (1,)), ((), ()))


def hops(step, ring):
    return min(step, ring - step)


LAT_STEPS = sorted(
    [(dx, dy) for dx in range(NX) for dy in range(NY) if dx + dy],
    key=lambda d: -hops(d[0], NX) - hops(d[1], NY),
)
CHAN_STEPS = sorted(
    [(dz, dc) for dz in range(NZ) for dc in range(2) if dz + dc],
    key=lambda d: -2 * hops(d[0], NZ) - d[1],
)


def fourier_table():
    orders = np.arange(ORDERS, dtype=np.int32)[:, None]
    columns = np.arange(NLON, dtype=np.int32)[None, :]
    phases = np.float32(2.0 * math.pi / NLON) * ((orders * columns) % NLON).astype(np.float32)
    return np.concatenate([np.cos(phases), -np.sin(phases)], axis=0).astype(ml_dtypes.bfloat16)


def constants():
    row = np.arange(N_LAT * ROWS)
    part, half, pair = (row // 12) % 2, (row // 6) % 2, (row // ROWS) * MINE + row % MINE
    pick = np.zeros((row.size, PAIRS), np.float32)
    pick[row, pair] = 1 - 2 * half
    base = np.broadcast_to((part * ORDERS + half * (ORDERS - 1))[:, None], (row.size, 128))
    s, t, c = np.meshgrid(np.arange(8), np.arange(LAT), np.arange(CH), indexing="ij")
    regroup = np.zeros((1024, 1024), np.float32)
    regroup[(s * 128 + t * CH + c).ravel(), (c * 128 + s * LAT + t).ravel()] = 1
    k, r, c = np.meshgrid(np.arange(MINE), np.arange(2), np.arange(CH), indexing="ij")
    arrange = np.zeros((CH * ROWS, CH * ROWS), np.float32)
    for half in range(2):
        arrange[(k * 32 + half * 16 + r * 8 + c).ravel(), (c * ROWS + r * 12 + half * MINE + k).ravel()] = 1
    out_row = np.arange(MINE * 16)
    offset = np.arange(PAIRS)[None, :] - (out_row // 16)[:, None]
    index = offset.astype(np.int32)
    bf = ml_dtypes.bfloat16
    return (
        fourier_table(),
        pick.astype(bf),
        base.astype(np.float32),
        regroup.astype(bf),
        arrange.astype(bf),
        index,
    )


def drain(buffer, sem):
    pltpu.make_async_copy(buffer, buffer, sem).wait()


def kernel(
    x_hbm, leg_hbm, mix_hbm, order_hbm, table_hbm, pick_hbm, base_hbm, regroup_hbm, arrange_hbm, index_hbm,
    out_ref,
    x, leg, turned_leg, order, table, pick, base, regroup, arrange, index,
    send, recv, weights, units, gathered, mixed, back,
    local_sem, lat_send, lat_recv, w_send, w_recv, c_send, c_recv, m_send, m_recv,
):
    li, ci = lax.axis_index("lat"), lax.axis_index("chan")
    loads = [
        pltpu.make_async_copy(src, dst, local_sem.at[i])
        for i, (src, dst) in enumerate(
            [
                (order_hbm, order), (pick_hbm, pick), (base_hbm, base), (x_hbm, x), (table_hbm.at[pl.ds(0, ORDERS)], table.at[pl.ds(0, ORDERS)]),
                (mix_hbm, weights.at[ci]), (index_hbm, index), (arrange_hbm, arrange), (regroup_hbm, regroup),
                (leg_hbm, leg), (table_hbm.at[pl.ds(ORDERS, ORDERS)], table.at[pl.ds(ORDERS, ORDERS)]),
            ]
        )
    ]
    lx, ly, cz, cc = lax.div(li, NY), lax.rem(li, NY), lax.div(ci, 2), lax.rem(ci, 2)
    xs = [lax.rem(lx + d, NX) * NY for d in range(NX)]
    ys = [lax.rem(ly + d, NY) for d in range(NY)]
    zs = [lax.rem(cz + d, NZ) * 2 for d in range(NZ)]
    cs = [lax.rem(cc + d, 2) for d in range(2)]
    lat_peers = [xs[dx] + ys[dy] for dx, dy in LAT_STEPS]
    chan_peers = [zs[dz] + cs[dc] for dz, dc in CHAN_STEPS]

    for load in loads[:5]:
        load.start()
    barrier = pltpu.get_barrier_semaphore()
    far = [(hops(dx, NX) + hops(dy, NY), peer, ci) for (dx, dy), peer in zip(LAT_STEPS, lat_peers)]
    far += [(hops(dz, NZ), li, peer) for (dz, dc), peer in zip(CHAN_STEPS, chan_peers)]
    for _, lat, chan in sorted(far, key=lambda f: -f[0]):
        pl.semaphore_signal(barrier, inc=1, device_id=(lat, chan), device_id_type=MESH)
    for load in loads[10:] + loads[5:10]:
        load.start()
    for load in loads[:3]:
        load.wait()
    order_rows = jnp.broadcast_to(order[...], (128, PAIRS)).astype(F32).astype(BF16)
    key = base[...] + lax.dot_general(pick[...], order_rows, NT, preferred_element_type=F32)
    column = lax.broadcasted_iota(jnp.int32, key.shape, 1).astype(F32)
    place = jnp.concatenate(
        [jnp.where(key == column + 128.0 * b, 1.0, 0.0).astype(BF16) for b in range(2 * ORDERS // 128)],
        axis=1,
    )
    loads[3].wait()
    parts = []
    for load, part in ((loads[4], 0), (loads[10], 1)):
        load.wait()
        rows = table[part * ORDERS : (part + 1) * ORDERS]
        spectrum = lax.dot_general(rows, x[...], NT, preferred_element_type=F32)
        parts.append((spectrum * (1.0 / math.sqrt(NLON))).astype(BF16))
    placed = jnp.dot(place, jnp.concatenate(parts, axis=0), preferred_element_type=F32)
    send[...] = placed.reshape(N_LAT, ROWS, 128).astype(BF16)

    pl.semaphore_wait(barrier, N_LAT + N_CHAN - 2)

    for peer in lat_peers:
        pltpu.make_async_remote_copy(
            src_ref=send.at[peer], dst_ref=recv.at[li], send_sem=lat_send.at[0], recv_sem=lat_recv.at[0],
            device_id=(peer, ci), device_id_type=MESH,
        ).start()
    pltpu.make_async_copy(send.at[li], recv.at[li], lat_recv.at[0]).start()
    loads[5].wait()
    for peer in chan_peers:
        pltpu.make_async_remote_copy(
            src_ref=weights.at[ci], dst_ref=weights.at[ci], send_sem=w_send.at[0], recv_sem=w_recv.at[0],
            device_id=(li, peer), device_id_type=MESH,
        ).start()

    for load in loads[6:10]:
        load.wait()
    mine = jnp.where(index[...] == li * MINE, 1.0, 0.0).astype(BF16)
    my_order = lax.dot_general(mine, order_rows, NT, preferred_element_type=F32)
    first = lax.broadcasted_iota(jnp.int32, (MINE * 16, SLOTS), 1).astype(F32) < (
        float(ORDERS) - my_order[:, 0:1]
    )

    lat_ids = [lax.broadcasted_iota(jnp.int32, (N_LAT * LAT, N_LAT * LAT), d) for d in range(2)]
    unit = jnp.where(lat_ids[0] == lat_ids[1], 1.0, 0.0).astype(BF16)
    for k in range(MINE):
        turned_leg[k] = lax.dot_general(unit, leg[k], NT, preferred_element_type=F32).astype(BF16)

    drain(recv, lat_recv.at[0])
    blocks = jnp.concatenate(
        [
            jnp.concatenate([recv[g * 8 + s].astype(F32) for s in range(8)], axis=1)
            for g in range(N_LAT // 8)
        ],
        axis=0,
    ).astype(BF16)
    turned = jnp.dot(blocks, regroup[...], preferred_element_type=F32)
    fields = jnp.concatenate(
        [
            jnp.concatenate(
                [turned[g * ROWS : (g + 1) * ROWS, c * 128 : (c + 1) * 128] for g in range(N_LAT // 8)],
                axis=1,
            )
            for c in range(CH)
        ],
        axis=0,
    ).astype(BF16)
    fields = jnp.dot(arrange[...], fields, preferred_element_type=F32).astype(BF16)
    ends = jnp.zeros((16, 128), F32)
    end_lane = lax.broadcasted_iota(jnp.int32, (16, 128), 1)
    for k in range(MINE):
        sums = jnp.dot(fields[k * 32 : (k + 1) * 32], turned_leg[k], preferred_element_type=F32)
        piece = jnp.where(first[k * 16 : (k + 1) * 16], sums[0:16], sums[16:32])
        for b in range(3):
            units[k * 3 + b] = piece[:, b * 128 : (b + 1) * 128].astype(BF16)
        ends = jnp.where(end_lane == k, jnp.broadcast_to(piece[:, ORDERS:], (16, 128)), ends)
    units[UNITS - 1] = ends.astype(BF16)

    def extra_copy(e):
        return pltpu.make_async_remote_copy(
            src_ref=units.at[N_CHAN + e], dst_ref=gathered.at[1, ci], send_sem=c_send.at[1 + e],
            recv_sem=c_recv.at[1], device_id=(li, e * APART), device_id_type=MESH,
        )

    def keep_unit(unit, slot):
        return pltpu.make_async_copy(units.at[unit], gathered.at[slot, ci], c_recv.at[slot])

    def send_back(unit, slot):
        for peer in chan_peers:
            pltpu.make_async_remote_copy(
                src_ref=mixed.at[slot, peer], dst_ref=back.at[unit], send_sem=m_send.at[slot],
                recv_sem=m_recv.at[0], device_id=(li, peer), device_id_type=MESH,
            ).start()
        pltpu.make_async_copy(mixed.at[slot, ci], back.at[unit], m_recv.at[0]).start()

    for e in range(UNITS - N_CHAN):

        @pl.when(ci != e * APART)
        def _():
            extra_copy(e).start()

        @pl.when(ci == e * APART)
        def _():
            keep_unit(N_CHAN + e, 1).start()

    for peer in chan_peers:
        pltpu.make_async_remote_copy(
            src_ref=units.at[peer], dst_ref=gathered.at[0, ci], send_sem=c_send.at[0],
            recv_sem=c_recv.at[0], device_id=(li, peer), device_id_type=MESH,
        ).start()
    keep_unit(ci, 0).start()

    drain(weights.at[pl.ds(0, N_CHAN - 1)], w_recv.at[0])
    every = weights[...].astype(F32).reshape(N_CHAN, 2, CH, 128)
    w_real = every[:, 0].reshape(128, 128)
    w_imag = every[:, 1].reshape(128, 128)
    to_real = jnp.concatenate([w_real, -w_imag], axis=1).astype(BF16)
    to_imag = jnp.concatenate([w_imag, w_real], axis=1).astype(BF16)
    drain(send.at[pl.ds(0, N_LAT - 1)], lat_send.at[0])
    drain(weights.at[pl.ds(0, N_CHAN - 1)], w_send.at[0])

    drain(gathered.at[0], c_recv.at[0])
    for e in range(UNITS - N_CHAN):

        @pl.when(ci == e * APART)
        def _():
            drain(gathered.at[1], c_recv.at[1])

    both = gathered[...].astype(F32).reshape(2, N_CHAN, 2, CH, 128)
    both = jnp.concatenate(
        [
            jnp.concatenate([both[slot, :, part].reshape(128, 128) for slot in range(2)], axis=1)
            for part in range(2)
        ],
        axis=0,
    ).astype(BF16)
    real = jnp.dot(to_real, both, preferred_element_type=F32)
    imag = jnp.dot(to_imag, both, preferred_element_type=F32)
    for slot in range(2):
        parts = [
            whole[:, slot * 128 : (slot + 1) * 128].reshape(N_CHAN, CH, 128) for whole in (real, imag)
        ]
        mixed[slot] = jnp.concatenate(parts, axis=1).astype(BF16)

    for e in range(UNITS - N_CHAN):

        @pl.when(ci == e * APART)
        def _():
            send_back(N_CHAN + e, 1)

    send_back(ci, 0)

    drain(units.at[pl.ds(0, N_CHAN - 1)], c_send.at[0])
    for e in range(UNITS - N_CHAN):

        @pl.when(ci != e * APART)
        def _():
            extra_copy(e).wait_send()

    drain(back, m_recv.at[0])
    last = back[UNITS - 1].astype(F32)
    for k in range(MINE):
        out_ref[k] = jnp.concatenate(
            [back[k * 3 + b].astype(F32) for b in range(3)] + [last[:, k : k + 1]], axis=1
        ).astype(BF16)

    drain(mixed.at[0, pl.ds(0, N_CHAN - 1)], m_send.at[0])
    for e in range(UNITS - N_CHAN):

        @pl.when(ci == e * APART)
        def _():
            drain(mixed.at[1, pl.ds(0, N_CHAN - 1)], m_send.at[1])


def body(grid_field, legendre, mix_weight, pair_order):
    any_spec = pl.BlockSpec(memory_space=pl.ANY)
    dma = pltpu.SemaphoreType.DMA
    fixed = [jnp.asarray(c) for c in constants()]
    out = pl.pallas_call(
        kernel,
        out_shape=pltpu.VMEM((MINE, 16, SLOTS), BF16),
        in_specs=[any_spec] * 10,
        out_specs=pl.BlockSpec(memory_space=pltpu.VMEM),
        scratch_shapes=[
            pltpu.VMEM((LAT * CH, NLON), BF16),
            pltpu.VMEM((MINE, SLOTS, N_LAT * LAT), BF16),
            pltpu.VMEM((MINE, N_LAT * LAT, SLOTS), BF16),
            pltpu.VMEM((1, PAIRS), jnp.int32),
            pltpu.VMEM((2 * ORDERS, NLON), BF16),
            pltpu.VMEM((N_LAT * ROWS, PAIRS), BF16),
            pltpu.VMEM((N_LAT * ROWS, 128), F32),
            pltpu.VMEM((1024, 1024), BF16),
            pltpu.VMEM((CH * ROWS, CH * ROWS), BF16),
            pltpu.VMEM((MINE * 16, PAIRS), jnp.int32),
            pltpu.VMEM((N_LAT, ROWS, 128), BF16),
            pltpu.VMEM((N_LAT, ROWS, 128), BF16),
            pltpu.VMEM((N_CHAN, 16, 128), BF16),
            pltpu.VMEM((UNITS, 16, 128), BF16),
            pltpu.VMEM((2, N_CHAN, 16, 128), BF16),
            pltpu.VMEM((2, N_CHAN, 16, 128), BF16),
            pltpu.VMEM((UNITS, 16, 128), BF16),
            dma((11,)),
            dma((1,)),
            dma((1,)),
            dma((1,)),
            dma((1,)),
            dma((1 + UNITS - N_CHAN,)),
            dma((2,)),
            dma((2,)),
            dma((1,)),
        ],
        compiler_params=pltpu.CompilerParams(
            collective_id=0, has_side_effects=True, vmem_limit_bytes=60 * 1024 * 1024
        ),
    )(
        grid_field.reshape(LAT * CH, NLON),
        jnp.transpose(legendre, (1, 2, 0)),
        mix_weight.reshape(16, 128),
        pair_order.reshape(1, PAIRS),
        *fixed,
    )
    return out.reshape(MINE, 2, CH, SLOTS)


def solution(mesh):
    return jax.shard_map(
        body,
        mesh=mesh,
        in_specs=(P("lat", "chan", None), P(None, "lat", None), P(None, "chan", None), P()),
        out_specs=P("lat", None, "chan", None),
        check_vma=False,
    )
```
